32 devices in a mesh: dp: 4 (over y, x), fsdp: 8 (over z, core).
Axes of the slice: x: 2, y: 2, z: 4, core: 2. Of those that a mesh axis runs over, the one named last changes fastest.
Arguments:
- tokens: bfloat16 [64, 64, 1536], P(('dp', 'fsdp')), may hold values from -6 to 6
- cotangent: bfloat16 [64, 64, 1536], P(('dp', 'fsdp')), may hold values from -6 to 6
- lengths: int32 [64], P(('dp', 'fsdp')), may hold values from 16 to 64, as said below
- in_proj: float32 [1536, 3072], P(None, ('dp', 'fsdp')), may hold values from -0.15625 to 0.15625
- out_proj: float32 [1536, 1536], P(None, ('dp', 'fsdp')), may hold values from -0.875 to 0.875
- gate_up: float32 [2, 1536, 4096], P(None, None, ('dp', 'fsdp')), may hold values from -0.15625 to 0.15625
- down_proj: float32 [4096, 1536], P(('dp', 'fsdp')), may hold values from -0.09375 to 0.09375
- gains_pair: float32 [2, 1536], P(None, ('dp', 'fsdp')), may hold values from 0.5 to 1.5
- in_proj_mom: float32 [1536, 3072], P(None, ('dp', 'fsdp')), may hold values from -96 to 96
- out_proj_mom: float32 [1536, 1536], P(None, ('dp', 'fsdp')), may hold values from -96 to 96
- gate_up_mom: float32 [2, 1536, 4096], P(None, None, ('dp', 'fsdp')), may hold values from -96 to 96
- down_proj_mom: float32 [4096, 1536], P(('dp', 'fsdp')), may hold values from -96 to 96
- gains_mom: float32 [2, 1536], P(None, ('dp', 'fsdp')), may hold values from -96 to 96
- in_proj_avg: float32 [1536, 3072], P(None, ('dp', 'fsdp')), may hold values from -0.15625 to 0.15625
- out_proj_avg: float32 [1536, 1536], P(None, ('dp', 'fsdp')), may hold values from -0.875 to 0.875
- gate_up_avg: float32 [2, 1536, 4096], P(None, None, ('dp', 'fsdp')), may hold values from -0.15625 to 0.15625
- down_proj_avg: float32 [4096, 1536], P(('dp', 'fsdp')), may hold values from -0.09375 to 0.09375
- gains_avg: float32 [2, 1536], P(None, ('dp', 'fsdp')), may hold values from 0.5 to 1.5
Outputs:
- output: bfloat16 [64, 64, 1536], P(('dp', 'fsdp'))
- input_grad: float32 [64, 64, 1536], P(('dp', 'fsdp'))
- in_proj_grad: float32 [1536, 3072], P(None, ('dp', 'fsdp'))
- in_proj_mom_new: float32 [1536, 3072], P(None, ('dp', 'fsdp'))
- in_proj_new: float32 [1536, 3072], P(None, ('dp', 'fsdp'))
- in_proj_avg_new: float32 [1536, 3072], P(None, ('dp', 'fsdp'))
- in_proj_copy: bfloat16 [1536, 3072], P(None, ('dp', 'fsdp'))
- out_proj_grad: float32 [1536, 1536], P(None, ('dp', 'fsdp'))
- out_proj_mom_new: float32 [1536, 1536], P(None, ('dp', 'fsdp'))
- out_proj_new: float32 [1536, 1536], P(None, ('dp', 'fsdp'))
- out_proj_avg_new: float32 [1536, 1536], P(None, ('dp', 'fsdp'))
- out_proj_copy: bfloat16 [1536, 1536], P(None, ('dp', 'fsdp'))
- gate_up_grad: float32 [2, 1536, 4096], P(None, None, ('dp', 'fsdp'))
- gate_up_mom_new: float32 [2, 1536, 4096], P(None, None, ('dp', 'fsdp'))
- gate_up_new: float32 [2, 1536, 4096], P(None, None, ('dp', 'fsdp'))
- gate_up_avg_new: float32 [2, 1536, 4096], P(None, None, ('dp', 'fsdp'))
- gate_up_copy: bfloat16 [2, 1536, 4096], P(None, None, ('dp', 'fsdp'))
- down_proj_grad: float32 [4096, 1536], P(('dp', 'fsdp'))
- down_proj_mom_new: float32 [4096, 1536], P(('dp', 'fsdp'))
- down_proj_new: float32 [4096, 1536], P(('dp', 'fsdp'))
- down_proj_avg_new: float32 [4096, 1536], P(('dp', 'fsdp'))
- down_proj_copy: bfloat16 [4096, 1536], P(('dp', 'fsdp'))
- gains_grad: float32 [2, 1536], P(None, ('dp', 'fsdp'))
- gains_mom_new: float32 [2, 1536], P(None, ('dp', 'fsdp'))
- gains_new: float32 [2, 1536], P(None, ('dp', 'fsdp'))
- gains_avg_new: float32 [2, 1536], P(None, ('dp', 'fsdp'))
- gains_copy: bfloat16 [2, 1536], P(None, ('dp', 'fsdp'))
The draws below stay inside these ranges and needn't reach their ends.
Inputs may be any that keep to these rules, and one draw needn't show every extreme that they name: `lengths`: valid tokens of each slot, counted from its start; both ends are reached.
All inputs are finite; a program needn't handle non-finite values.
Results may differ from the reference program's by a relative error of at most 0.014.
The reference program's roundings to bfloat16 on the way count: a program that leaves them out, or rounds other values in their place, can miss the bound.
Values may be sent and summed in bfloat16 or wider, within the bound.
No kernel may reach another device: no remote copies, remote signals or barrier semaphores. Data moves between devices by JAX's collectives and lax.ppermute only.
A program may use at most 512 MiB of HBM per device.

```python
import math
import jax
import jax.numpy as jnp
from jax import lax

D = 1536
HEADS = 16
KV_HEADS = 8
HEAD_DIM = 96
FF = 4096
SLOT = 64
SLOTS = 64


def draw_lengths(key, part):
    key = jax.random.fold_in(key, 11)
    key_lens, key_pick = jax.random.split(key)
    values = jax.random.randint(key_lens, (SLOTS,), SLOT // 4, SLOT + 1)
    picked = jax.random.permutation(key_pick, SLOTS)
    values = values.at[picked[0]].set(SLOT)
    values = values.at[picked[1]].set(SLOT // 4)
    return values.astype(jnp.int32)


def block_levels(stream_key, extent, cuts, low, high):
    level = 1.0
    for position, shards_of in cuts:
        draws = jax.random.uniform(jax.random.fold_in(jax.random.fold_in(stream_key, 6), position), (shards_of,), jnp.float32, low / len(cuts), high / len(cuts))
        level = level * jnp.repeat(jnp.exp(draws), extent[position] // shards_of).reshape((-1,) + (1,) * (len(extent) - 1 - position))
    return level


def scatter_about(key, extent, scale, reach, cuts=(), kind=jnp.bfloat16):
    array = scale * jax.random.normal(key, extent, jnp.float32)
    if cuts:
        array = array * block_levels(key, extent, cuts, -0.22, 0.18)
    return jnp.clip(array, -reach, reach).astype(kind)


def setup_inputs(seed: int = 0) -> dict:
    streams_of = jax.random.split(jax.random.key(seed), 19)
    tokens = scatter_about(streams_of[0], (SLOTS, SLOT, D), 1.0, 6.0, ((0, 32),))
    cotangent = scatter_about(streams_of[1], (SLOTS, SLOT, D), 1.0, 6.0, ((0, 32),))
    lengths = draw_lengths(jax.random.fold_in(streams_of[18], 71), 0)
    in_proj = scatter_about(streams_of[3], (D, D + 2 * KV_HEADS * HEAD_DIM), D ** -0.5, 0.15625, ((1, 32),), jnp.float32)
    out_proj = scatter_about(streams_of[4], (D, D), (D // 32) ** -0.5, 0.875, ((1, 32),), jnp.float32)
    gate_up = scatter_about(streams_of[5], (2, D, FF), D ** -0.5, 0.15625, ((2, 32),), jnp.float32)
    down_proj = scatter_about(streams_of[6], (FF, D), FF ** -0.5, 0.09375, ((0, 32),), jnp.float32)
    gains_pair = jnp.clip(1.0 + 0.1 * jax.random.normal(streams_of[7], (2, D), jnp.float32), 0.5, 1.5)
    in_proj_mom = scatter_about(streams_of[8], (D, D + 2 * KV_HEADS * HEAD_DIM), ((SLOTS * SLOT) ** 0.5 / 4), 96.0, ((1, 32),), jnp.float32)
    out_proj_mom = scatter_about(streams_of[9], (D, D), ((SLOTS * SLOT) ** 0.5 / 4), 96.0, ((1, 32),), jnp.float32)
    gate_up_mom = scatter_about(streams_of[10], (2, D, FF), ((SLOTS * SLOT) ** 0.5 / 4), 96.0, ((2, 32),), jnp.float32)
    down_proj_mom = scatter_about(streams_of[11], (FF, D), ((SLOTS * SLOT) ** 0.5 / 4), 96.0, ((0, 32),), jnp.float32)
    gains_mom = scatter_about(streams_of[12], (2, D), ((SLOTS * SLOT) ** 0.5 / 4), 96.0, ((1, 32),), jnp.float32)
    in_proj_avg = scatter_about(streams_of[13], (D, D + 2 * KV_HEADS * HEAD_DIM), D ** -0.5, 0.15625, ((1, 32),), jnp.float32)
    out_proj_avg = scatter_about(streams_of[14], (D, D), (D // 32) ** -0.5, 0.875, ((1, 32),), jnp.float32)
    gate_up_avg = scatter_about(streams_of[15], (2, D, FF), D ** -0.5, 0.15625, ((2, 32),), jnp.float32)
    down_proj_avg = scatter_about(streams_of[16], (FF, D), FF ** -0.5, 0.09375, ((0, 32),), jnp.float32)
    gains_avg = jnp.clip(1.0 + 0.1 * jax.random.normal(streams_of[17], (2, D), jnp.float32), 0.5, 1.5)
    return dict(tokens=tokens, cotangent=cotangent, lengths=lengths, in_proj=in_proj, out_proj=out_proj, gate_up=gate_up, down_proj=down_proj, gains_pair=gains_pair, in_proj_mom=in_proj_mom, out_proj_mom=out_proj_mom, gate_up_mom=gate_up_mom, down_proj_mom=down_proj_mom, gains_mom=gains_mom, in_proj_avg=in_proj_avg, out_proj_avg=out_proj_avg, gate_up_avg=gate_up_avg, down_proj_avg=down_proj_avg, gains_avg=gains_avg)


EPS = 1e-05
THETA = 10000.0
MASKED = -1e+30
MOMENTUM_RATE = 0.9
AVERAGE_RATE = 0.75
RATE_BASE = 0.1
HIGH = lax.Precision.HIGHEST

@jax.custom_vjp
def low(v):
    return lax.optimization_barrier(v.astype(jnp.bfloat16)).astype(jnp.float32)

@jax.custom_vjp
def low_back(v):
    return v

def low_keep(v):
    return (low(v), None)

def low_pass(kept, grad):
    return (grad,)

def back_keep(v):
    return (v, None)

def back_low(kept, grad):
    return (low(grad),)
low.defvjp(low_keep, low_pass)
low_back.defvjp(back_keep, back_low)

def rotary_tables(seq_len):
    positions = jnp.arange(seq_len, dtype=jnp.float32)
    halves = jnp.arange(HEAD_DIM // 2, dtype=jnp.float32)
    frequencies = jnp.power(THETA, -2.0 * halves / HEAD_DIM)
    angles = positions[:, None] * frequencies[None, :]
    return (jnp.cos(angles), jnp.sin(angles))

def rotate(values, cos_table, sine_table):
    half_width = values.shape[-1] // 2
    first_half = values[..., :half_width]
    second_half = values[..., half_width:]
    cos_part = cos_table[:, None, :]
    sine_part = sine_table[:, None, :]
    return jnp.concatenate([first_half * cos_part - second_half * sine_part, second_half * cos_part + first_half * sine_part], axis=-1)

def rms_scale(values):
    return lax.rsqrt(lax.optimization_barrier(jnp.mean(values * values, axis=-1, keepdims=True)) + EPS)

def slot_forward(inputs, length, in_full, out_full, gate_full, down_full, gain_pair):
    seq_len = inputs.shape[0]
    kv_width = KV_HEADS * HEAD_DIM
    groups = HEADS // KV_HEADS
    positions = jnp.arange(seq_len)
    is_valid = positions < length
    normed = low(inputs * rms_scale(inputs) * gain_pair[0])
    projected = low_back(jnp.dot(normed, in_full, precision=HIGH))
    cos_table, sine_table = rotary_tables(seq_len)
    queries = low(rotate(projected[:, :D].reshape(seq_len, HEADS, HEAD_DIM), cos_table, sine_table))
    queries = queries.reshape(seq_len, KV_HEADS, groups, HEAD_DIM)
    key_rows = low(rotate(projected[:, D:D + kv_width].reshape(seq_len, KV_HEADS, HEAD_DIM), cos_table, sine_table))
    value_rows = low(projected[:, D + kv_width:].reshape(seq_len, KV_HEADS, HEAD_DIM))
    scores = low_back(jnp.einsum('skgd,tkd->kgst', queries, key_rows, precision=HIGH) * HEAD_DIM ** (-0.5))
    allowed = (positions[None, :] <= positions[:, None]) & is_valid[None, :]
    masked = jnp.where(allowed, scores, MASKED)
    row_max = lax.optimization_barrier(jnp.max(masked, axis=-1, keepdims=True))
    exps = jnp.exp(masked - row_max)
    probabilities = low(exps / lax.optimization_barrier(jnp.sum(exps, axis=-1, keepdims=True)))
    attended = jnp.einsum('kgst,tkd->skgd', probabilities, value_rows, precision=HIGH).reshape(seq_len, D)
    attended = low(low_back(attended))
    hidden = inputs + low_back(jnp.dot(attended, out_full, precision=HIGH))
    normed_two = low(hidden * rms_scale(hidden) * gain_pair[1])
    gate_part = low_back(jnp.dot(normed_two, gate_full[0], precision=HIGH))
    up_part = low_back(jnp.dot(normed_two, gate_full[1], precision=HIGH))
    active = low(gate_part * jax.nn.sigmoid(gate_part) * up_part)
    result = hidden + low_back(jnp.dot(active, down_full, precision=HIGH))
    return jnp.where(is_valid[:, None], result, 0.0)

def reference(tokens, cotangent, lengths, in_proj, out_proj, gate_up, down_proj, gains_pair, in_proj_mom, out_proj_mom, gate_up_mom, down_proj_mom, gains_mom, in_proj_avg, out_proj_avg, gate_up_avg, down_proj_avg, gains_avg):
    masters = (in_proj, out_proj, gate_up, down_proj, gains_pair)
    rounded = tuple((lax.optimization_barrier(weight.astype(jnp.bfloat16)).astype(jnp.float32) for weight in masters))
    group_size = max(1, min(SLOTS, 4096 // SLOT))
    group_count = SLOTS // group_size
    token_groups = tokens.astype(jnp.float32).reshape(group_count, group_size, SLOT, D)
    upstream_groups = cotangent.astype(jnp.float32).reshape(group_count, group_size, SLOT, D)
    length_groups = lengths.reshape(group_count, group_size)

    def group_step(totals, batch):
        inputs, upstream, group_lengths = batch

        def run_group(group_inputs, weights):

            def single(one_slot, one_length):
                return slot_forward(one_slot, one_length, weights[0], weights[1], weights[2], weights[3], weights[4])
            return jax.vmap(single)(group_inputs, group_lengths)
        results, pullback = jax.vjp(run_group, inputs, rounded)
        grad_inputs, grad_weights = pullback(upstream)
        totals = tuple((total + gradient for total, gradient in zip(totals, grad_weights)))
        return (totals, (results.astype(jnp.bfloat16), grad_inputs))
    zeros = tuple((jnp.zeros_like(weight) for weight in masters))
    totals, (outputs, grad_inputs) = lax.scan(group_step, zeros, (token_groups, upstream_groups, length_groups))
    step_rate = RATE_BASE / math.sqrt(SLOTS * SLOT)

    def update(weight, gradient, moment, average):
        moment_new = MOMENTUM_RATE * moment + gradient
        weight_new = weight - step_rate * (gradient + MOMENTUM_RATE * moment_new)
        average_new = AVERAGE_RATE * average + (1.0 - AVERAGE_RATE) * weight_new
        return (gradient, moment_new, weight_new, average_new, weight_new.astype(jnp.bfloat16))
    in_g, in_m, in_w, in_a, in_c = update(in_proj, totals[0], in_proj_mom, in_proj_avg)
    out_g, out_m, out_w, out_a, out_c = update(out_proj, totals[1], out_proj_mom, out_proj_avg)
    gu_g, gu_m, gu_w, gu_a, gu_c = update(gate_up, totals[2], gate_up_mom, gate_up_avg)
    dn_g, dn_m, dn_w, dn_a, dn_c = update(down_proj, totals[3], down_proj_mom, down_proj_avg)
    gn_g, gn_m, gn_w, gn_a, gn_c = update(gains_pair, totals[4], gains_mom, gains_avg)
    return (outputs.reshape(SLOTS, SLOT, D), grad_inputs.reshape(SLOTS, SLOT, D), in_g, in_m, in_w, in_a, in_c, out_g, out_m, out_w, out_a, out_c, gu_g, gu_m, gu_w, gu_a, gu_c, dn_g, dn_m, dn_w, dn_a, dn_c, gn_g, gn_m, gn_w, gn_a, gn_c)
```

```python
import math

import jax
import jax.numpy as jnp
from jax import lax
from jax.sharding import PartitionSpec as P

D = 1536
HEADS = 16
KV_HEADS = 8
HEAD_DIM = 96
ALL_HEADS = HEADS + 2 * KV_HEADS
GROUPS = HEADS // KV_HEADS

EPS = 1e-05
THETA = 10000.0
MASKED = -1e30
MOMENTUM_RATE = 0.9
AVERAGE_RATE = 0.75
RATE_BASE = 0.1
AXES = ("dp", "fsdp")
LEFT_ROWS = (((0,), (0,)), ((), ()))
RIGHT_ROWS = (((1,), (1,)), ((), ()))


def rotary_tables(seq_len):
    positions = jnp.arange(seq_len, dtype=jnp.float32)
    halves = jnp.arange(HEAD_DIM // 2, dtype=jnp.float32)
    frequencies = jnp.power(THETA, -2.0 * halves / HEAD_DIM)
    angles = positions[:, None] * frequencies[None, :]
    return (jnp.cos(angles), jnp.sin(angles))


def turn(values, cos_part, sine_part):
    half_width = values.shape[-1] // 2
    first_half = values[..., :half_width]
    second_half = values[..., half_width:]
    return jnp.concatenate(
        [
            first_half * cos_part - second_half * sine_part,
            second_half * cos_part + first_half * sine_part,
        ],
        axis=-1,
    )


def rms_scale(values):
    return lax.rsqrt(jnp.mean(values * values, axis=-1, keepdims=True) + EPS)


def low(values):
    return values.astype(jnp.bfloat16)


def wide(values):
    return values.astype(jnp.float32)


def mm(a, b):
    return jnp.dot(a, b, preferred_element_type=jnp.float32)


def mm_left(a, b):
    return lax.dot_general(a, b, LEFT_ROWS, preferred_element_type=jnp.float32)


def mm_right(a, b):
    return lax.dot_general(a, b, RIGHT_ROWS, preferred_element_type=jnp.float32)


def update(weight, gradient, moment, average, step_rate):
    moment_new = MOMENTUM_RATE * moment + gradient
    weight_new = weight - step_rate * (gradient + MOMENTUM_RATE * moment_new)
    average_new = AVERAGE_RATE * average + (1.0 - AVERAGE_RATE) * weight_new
    return (gradient, moment_new, weight_new, average_new, weight_new.astype(jnp.bfloat16))


def flip_bits(values, axis, index):
    count = values.shape[axis]
    bit = 1
    while bit < count:
        shape = values.shape
        split = shape[:axis] + (count // (2 * bit), 2, bit) + shape[axis + 1 :]
        parts = values.reshape(split)
        flipped = jnp.flip(parts, axis + 1)
        values = jnp.where((index & bit) != 0, flipped, parts).reshape(shape)
        bit *= 2
    return values


class Links:
    def __init__(self, n_dp, n_fsdp):
        self.n_dp, self.n_z, self.count = n_dp, n_fsdp // 2, n_dp * n_fsdp
        self.dp = [n_fsdp * k for k in range(n_dp)]
        self.z = [2 * k for k in range(self.n_z)]
        assert n_dp & (n_dp - 1) == 0 and n_fsdp & (n_fsdp - 1) == 0

    def send(self, values, mask):
        return lax.ppermute(values, AXES, [(i, i ^ mask) for i in range(self.count)])

    def gather(self, values, masks):
        return jnp.stack([values] + [self.send(values, m) for m in masks[1:]])

    def gather_pair(self, values, masks):
        own = self.gather(values, masks)
        return jnp.stack([own, self.send(own, 1)])

    def spread(self, blocks, masks):
        return jnp.stack([blocks[0]] + [self.send(blocks[k], m) for k, m in enumerate(masks) if k])

    def spread_pair(self, blocks, masks):
        moved = jnp.stack([blocks[0], self.send(blocks[1], 1)])
        moved = jnp.swapaxes(moved, 0, 1)
        return jnp.swapaxes(self.spread(moved, masks), 0, 1)

    def add_up(self, blocks, masks):
        total = blocks[0]
        for k, m in enumerate(masks):
            if k:
                total = total + wide(self.send(low(blocks[k]), m))
        return total

    def add_up_pair(self, blocks, masks):
        mine = blocks[0] + wide(self.send(low(blocks[1]), 1))
        return self.add_up(mine, masks)


def on_device(
    tokens,
    cotangent,
    lengths,
    in_proj,
    out_proj,
    gate_up,
    down_proj,
    gains_pair,
    in_proj_mom,
    out_proj_mom,
    gate_up_mom,
    down_proj_mom,
    gains_mom,
    in_proj_avg,
    out_proj_avg,
    gate_up_avg,
    down_proj_avg,
    gains_avg,
):
    n_dp, n_fsdp = lax.axis_size("dp"), lax.axis_size("fsdp")
    links = Links(n_dp, n_fsdp)
    n_z, devices = links.n_z, links.count
    at_dp, at_fsdp = lax.axis_index("dp"), lax.axis_index("fsdp")
    at_z, at_core = at_fsdp // 2, at_fsdp % 2
    slots, seq_len = tokens.shape[:2]
    rows = slots * seq_len
    members = 2 * n_dp
    group_rows = 2 * n_z
    step_rate = RATE_BASE / math.sqrt(slots * devices * seq_len)
    inv_root = HEAD_DIM ** (-0.5)
    in_width = in_proj.shape[1]
    out_width = out_proj.shape[1]
    ff_width = down_proj.shape[0]

    in_low = low(jnp.transpose(in_proj))
    out_low = low(jnp.transpose(out_proj))
    gate_low = low(gate_up)
    down_low = low(down_proj)
    gain_low = low(gains_pair)

    gain_parts = links.gather_pair(links.gather(gain_low, links.z), links.dp)
    gain_parts = jnp.transpose(gain_parts, (1, 2, 0, 3, 4))
    gain_parts = gain_parts.reshape(devices, -1)
    at = at_dp * n_fsdp + at_fsdp
    one_hot = (jnp.arange(devices)[:, None] ^ at) == jnp.arange(devices)[None, :]
    gain_all = mm(low(one_hot), gain_parts).reshape(devices, 2, -1)
    gain_one = gain_all[:, 0].reshape(-1)
    gain_two = gain_all[:, 1].reshape(-1)

    token_rows = tokens.reshape(rows, D)
    token_group = links.gather_pair(token_rows, links.dp).reshape(members * rows, D)
    in_group = links.gather(in_low, links.z).reshape(n_z * in_width, D)
    out_full_t = lax.all_gather(out_low, AXES, axis=0, tiled=True)

    inputs_group = wide(token_group)
    unit_group = inputs_group * rms_scale(inputs_group)
    normed_group = low(unit_group * gain_one)
    projected = mm_right(normed_group, in_group)
    cos_table, sine_table = rotary_tables(seq_len)
    whole_heads = in_width == HEAD_DIM
    if whole_heads:
        heads = projected.reshape(members * slots, seq_len, n_z, HEAD_DIM)
        head_base = at_dp * n_fsdp
        turned = head_base < HEADS + KV_HEADS
        cos_here = jnp.where(turned, cos_table, 1.0)[:, None, :]
        sine_here = jnp.where(turned, sine_table, 0.0)[:, None, :]
        projected = low(turn(heads, cos_here, sine_here))
    blocks = projected.reshape(2, n_dp, rows, n_z * in_width)
    blocks = links.spread_pair(blocks, links.dp)
    blocks = blocks.reshape(2, n_dp, rows, n_z, in_width)
    blocks = jnp.transpose(blocks, (1, 3, 0, 2, 4))
    for axis, index in ((0, at_dp), (1, at_z), (2, at_core)):
        blocks = flip_bits(blocks, axis, index)
    blocks = blocks.reshape(devices, rows, in_width)
    if not whole_heads:
        blocks = jnp.transpose(blocks, (1, 0, 2)).reshape(rows, ALL_HEADS, HEAD_DIM)
        blocks = jnp.transpose(blocks, (1, 0, 2)).reshape(ALL_HEADS, slots, seq_len, HEAD_DIM)
        rotated = turn(blocks[: HEADS + KV_HEADS], cos_table, sine_table)
        blocks = low(jnp.concatenate([rotated, blocks[HEADS + KV_HEADS :]]))
    blocks = blocks.reshape(ALL_HEADS, slots, seq_len, HEAD_DIM)
    queries = blocks[:HEADS].reshape(KV_HEADS, GROUPS, slots, seq_len, HEAD_DIM)
    key_rows = blocks[HEADS : HEADS + KV_HEADS]
    value_rows = blocks[HEADS + KV_HEADS :]

    positions = jnp.arange(seq_len)
    is_valid = positions[None, :] < lengths[:, None]
    row_valid = is_valid.reshape(rows, 1)
    scores = (
        jnp.einsum("kgbsd,kbtd->kgbst", queries, key_rows, preferred_element_type=jnp.float32)
        * inv_root
    )
    allowed = (positions[None, :] <= positions[:, None])[None] & is_valid[:, None, :]
    masked = jnp.where(allowed, scores, MASKED)
    row_max = jnp.max(masked, axis=-1, keepdims=True)
    exps = jnp.exp(masked - row_max)
    probabilities = exps / jnp.sum(exps, axis=-1, keepdims=True)
    prob_low = low(probabilities)
    attended = jnp.einsum(
        "kgbst,kbtd->bskgd", prob_low, value_rows, preferred_element_type=jnp.float32
    )
    attended = low(attended).reshape(rows, D)
    inputs = wide(token_rows)
    hidden = inputs + mm_right(attended, out_full_t)
    scale_two = rms_scale(hidden)
    unit_two = hidden * scale_two
    normed_two = low(unit_two * gain_two)

    upstream = jnp.where(row_valid, cotangent.reshape(rows, D), jnp.zeros((), jnp.bfloat16))
    upstream_group = links.gather_pair(upstream, links.z).reshape(group_rows * rows, D)
    gate_group = links.gather(gate_low, links.dp)
    gate_w = jnp.transpose(gate_group, (1, 2, 0, 3)).reshape(2, D, n_dp * ff_width)
    down_w = links.gather(down_low, links.dp).reshape(n_dp * ff_width, D)
    normed_rows = links.gather_pair(normed_two, links.z).reshape(group_rows * rows, D)
    gate_part = mm(normed_rows, gate_w[0])
    up_part = mm(normed_rows, gate_w[1])
    sigmoid_gate = jax.nn.sigmoid(gate_part)
    silu_gate = gate_part * sigmoid_gate
    active = low(silu_gate * up_part)
    grad_active = mm_right(upstream_group, down_w)
    grad_gate = low(
        grad_active * up_part * sigmoid_gate * (1.0 + gate_part * (1.0 - sigmoid_gate))
    )
    grad_up = low(grad_active * silu_gate)
    grad_normed_two = mm_right(grad_gate, gate_w[0]) + mm_right(grad_up, gate_w[1])
    grad_normed_two = links.add_up_pair(
        grad_normed_two.reshape(2, n_z, rows, D), links.z
    )
    partial_out = mm(active, down_w)
    partial_out = links.add_up_pair(partial_out.reshape(2, n_z, rows, D), links.z)
    produced = low(jnp.where(row_valid, hidden + partial_out, 0.0))

    grad_gate_up = jnp.stack([mm_left(normed_rows, grad_gate), mm_left(normed_rows, grad_up)])
    grad_gate_up = jnp.moveaxis(grad_gate_up.reshape(2, D, n_dp, ff_width), 2, 0)
    grad_gate_up = links.add_up(grad_gate_up, links.dp)
    grad_down = mm_left(active, upstream_group).reshape(n_dp, ff_width, D)
    grad_down = links.add_up(grad_down, links.dp)

    gain_two_grad = jnp.sum(grad_normed_two * unit_two, axis=0)
    scaled_two = grad_normed_two * gain_two
    grad_hidden = wide(upstream) + scale_two * (
        scaled_two - unit_two * jnp.mean(scaled_two * unit_two, axis=-1, keepdims=True)
    )
    grad_branch = low(grad_hidden)
    grad_attended = low(mm(grad_branch, out_full_t))
    grad_attended = grad_attended.reshape(slots, seq_len, KV_HEADS, GROUPS, HEAD_DIM)
    grad_values = jnp.einsum(
        "kgbst,bskgd->kbtd", prob_low, grad_attended, preferred_element_type=jnp.float32
    )
    grad_probs = jnp.einsum(
        "bskgd,kbtd->kgbst", grad_attended, value_rows, preferred_element_type=jnp.float32
    )
    grad_scores = low(
        probabilities
        * (grad_probs - jnp.sum(probabilities * grad_probs, axis=-1, keepdims=True))
    )
    grad_queries = (
        jnp.einsum("kgbst,kbtd->kgbsd", grad_scores, key_rows, preferred_element_type=jnp.float32)
        * inv_root
    )
    grad_keys = (
        jnp.einsum("kgbst,kgbsd->kbtd", grad_scores, queries, preferred_element_type=jnp.float32)
        * inv_root
    )
    grad_heads = jnp.concatenate(
        [
            turn(grad_queries.reshape(HEADS, slots, seq_len, HEAD_DIM), cos_table, -sine_table),
            turn(grad_keys, cos_table, -sine_table),
            grad_values,
        ]
    )
    grad_heads = low(grad_heads).reshape(ALL_HEADS, rows, HEAD_DIM)
    if not whole_heads:
        grad_heads = jnp.transpose(grad_heads, (1, 0, 2)).reshape(rows, devices, in_width)
        grad_heads = jnp.transpose(grad_heads, (1, 0, 2))
    blocks = grad_heads.reshape(n_dp, n_z, 2, rows, in_width)
    for axis, index in ((0, at_dp), (1, at_z), (2, at_core)):
        blocks = flip_bits(blocks, axis, index)
    blocks = jnp.transpose(blocks, (2, 0, 3, 1, 4)).reshape(2, n_dp, rows, n_z * in_width)
    grad_proj = links.spread_pair(blocks, links.dp).reshape(members * rows, n_z * in_width)

    grad_in = mm_left(grad_proj, normed_group).reshape(n_z, in_width, D)
    grad_in = jnp.transpose(links.add_up(grad_in, links.z))
    grad_normed_one = mm(grad_proj, in_group).reshape(2, n_dp, rows, D)
    grad_normed_one = links.add_up_pair(grad_normed_one, links.dp)

    attended_group = links.gather_pair(attended, links.dp).reshape(members * rows, D)
    columns = jnp.transpose(grad_branch).reshape(n_dp, n_z, 2, out_width, rows)
    for axis, index in ((0, at_dp), (1, at_z), (2, at_core)):
        columns = flip_bits(columns, axis, index)
    columns = jnp.transpose(columns, (2, 0, 1, 3, 4)).reshape(2, n_dp, n_z * out_width, rows)
    columns = links.spread_pair(columns, links.dp).reshape(members, n_z * out_width, rows)
    columns = jnp.transpose(columns, (1, 0, 2)).reshape(n_z * out_width, members * rows)
    grad_out = mm(columns, attended_group).reshape(n_z, out_width, D)
    grad_out = jnp.transpose(links.add_up(grad_out, links.z))

    scale_one = rms_scale(inputs)
    unit_one = inputs * scale_one
    gain_one_grad = jnp.sum(grad_normed_one * unit_one, axis=0)
    scaled_one = grad_normed_one * gain_one
    grad_inputs = grad_hidden + scale_one * (
        scaled_one - unit_one * jnp.mean(scaled_one * unit_one, axis=-1, keepdims=True)
    )
    grad_gains = jnp.stack([gain_one_grad, gain_two_grad]).reshape(2, n_dp, n_z, 2, -1)
    grad_gains = jnp.transpose(grad_gains, (1, 2, 3, 0, 4)).reshape(devices, -1)
    grad_gains = jnp.dot(wide(one_hot), grad_gains, precision=lax.Precision.HIGHEST)
    grad_gains = grad_gains.reshape(n_dp, n_z, 2, 2, -1)
    total = grad_gains[:, :, 0] + links.send(grad_gains[:, :, 1], 1)
    total = total[0] + sum(links.send(total[k], m) for k, m in enumerate(links.dp) if k)
    grad_gain = total[0] + sum(links.send(total[k], m) for k, m in enumerate(links.z) if k)

    return (
        produced.reshape(tokens.shape),
        grad_inputs.reshape(tokens.shape),
        *update(in_proj, grad_in, in_proj_mom, in_proj_avg, step_rate),
        *update(out_proj, grad_out, out_proj_mom, out_proj_avg, step_rate),
        *update(gate_up, grad_gate_up, gate_up_mom, gate_up_avg, step_rate),
        *update(down_proj, grad_down, down_proj_mom, down_proj_avg, step_rate),
        *update(gains_pair, grad_gain, gains_mom, gains_avg, step_rate),
    )


def solution(mesh):
    rows = P(AXES, None, None)
    last_of_two = P(None, AXES)
    first_of_two = P(AXES, None)
    last_of_three = P(None, None, AXES)
    weights = (last_of_two, last_of_two, last_of_three, first_of_two, last_of_two)
    in_specs = (rows, rows, P(AXES)) + weights * 3
    out_specs = (rows, rows) + tuple(spec for spec in weights for _ in range(5))
    return jax.shard_map(
        on_device, mesh=mesh, in_specs=in_specs, out_specs=out_specs, check_vma=False
    )
```

```python
import functools
import math

import jax
import jax.numpy as jnp
from jax import lax
from jax.experimental import pallas as pl
from jax.experimental.pallas import tpu as pltpu
from jax.sharding import Mesh
from jax.sharding import PartitionSpec as P

D = 1536
HEADS = 16
KV_HEADS = 8
HEAD_DIM = 96
HALF = HEAD_DIM // 2
ALL_HEADS = HEADS + 2 * KV_HEADS
GROUPS = HEADS // KV_HEADS

EPS = 1e-05
THETA = 10000.0
MASKED = -1e30
MOMENTUM_RATE = 0.9
AVERAGE_RATE = 0.75
RATE_BASE = 0.1
AXES = ("dp", "z", "core")
PLANE = ("dp", "core")
NN = (((1,), (0,)), ((), ()))
TN = (((0,), (0,)), ((), ()))
NT = (((1,), (1,)), ((), ()))
VMEM_SLACK = 12 * 1024 * 1024
TILE = 256

bf16 = jnp.bfloat16
f32 = jnp.float32


def dot(a, b, dims):
    return lax.dot_general(a, b, dims, preferred_element_type=f32)


def low(values):
    return values.astype(bf16)


def wide(values):
    return values.astype(f32)


def rms_scale(values):
    return lax.rsqrt(jnp.mean(values * values, axis=-1, keepdims=True) + EPS)


def rotary_rows(seq_len, slots, heads):
    positions = jnp.arange(seq_len, dtype=f32)
    halves = jnp.arange(HALF, dtype=f32)
    frequencies = jnp.power(THETA, -2.0 * halves / HEAD_DIM)
    angles = positions[:, None] * frequencies[None, :]
    cos_table, sine_table = jnp.cos(angles), jnp.sin(angles)
    cos_rows = jnp.concatenate([cos_table, cos_table], axis=1)
    sine_rows = jnp.concatenate([-sine_table, sine_table], axis=1)
    return jnp.tile(cos_rows, (slots, heads)), jnp.tile(sine_rows, (slots, heads))


def swap_halves(values):
    width = values.shape[1]
    if width % 128 == 0:
        left = pltpu.roll(values, width - HALF, 1)
        right = pltpu.roll(values, HALF, 1)
    else:
        left = jnp.concatenate([values[:, HALF:], values[:, :HALF]], axis=1)
        right = jnp.concatenate([values[:, -HALF:], values[:, :-HALF]], axis=1)
    column = lax.broadcasted_iota(jnp.int32, values.shape, 1)
    return jnp.where(lax.rem(column, HEAD_DIM) < HALF, left, right)


def kernel_call(body, outs, ins, smem=(), hbm=(), scratch=(), sems=()):
    moved = [i for i in range(len(ins)) if i not in smem and i not in hbm]

    def fetched(*refs):
        given, rest = list(refs[: len(ins)]), refs[len(ins) :]
        held, sems = rest[-1 - len(moved) : -1], rest[-1]
        copies = [
            pltpu.make_async_copy(given[i], held[j], sems.at[j]) for j, i in enumerate(moved)
        ]
        for copy in copies:
            copy.start()
        for copy in copies:
            copy.wait()
        for j, i in enumerate(moved):
            given[i] = held[j]
        body(*given, *rest[: -1 - len(moved)])

    arrays = [*outs, *((ins[i].shape, ins[i].dtype) for i in moved)]
    arrays += scratch
    held_bytes = sum(math.prod(s) * jnp.dtype(t).itemsize for s, t in arrays)
    outputs = pl.pallas_call(
        fetched,
        out_shape=[jax.ShapeDtypeStruct(s, t) for s, t in outs],
        in_specs=[
            pl.BlockSpec(memory_space=pltpu.SMEM if i in smem else pltpu.HBM)
            for i in range(len(ins))
        ],
        out_specs=[pl.BlockSpec(memory_space=pltpu.VMEM)] * len(outs),
        scratch_shapes=[
            *(pltpu.VMEM(s, t) for s, t in scratch),
            *(pltpu.SemaphoreType.DMA(s) for s in sems),
            *(pltpu.VMEM(ins[i].shape, ins[i].dtype) for i in moved),
            pltpu.SemaphoreType.DMA((len(moved),)),
        ],
        compiler_params=pltpu.CompilerParams(vmem_limit_bytes=held_bytes + VMEM_SLACK),
        cost_estimate=pl.CostEstimate(flops=0, bytes_accessed=0, transcendentals=0),
    )(*ins)
    return list(outputs)


def project_body(x_ref, w_ref, gains_ref, cos_ref, sine_ref, out_ref, normed_ref, rows_ref):
    if gains_ref.shape[1] == D:
        rows_ref[...] = gains_ref[...]
    else:
        gains = wide(gains_ref[...])
        width = gains.shape[1] // 2
        for i in range(2):
            rows_ref[i : i + 1, :] = jnp.concatenate(
                [
                    gains[d : d + 1, i * width : (i + 1) * width]
                    for d in range(gains.shape[0])
                ],
                axis=1,
            )
    for k in range(x_ref.shape[0]):
        x = wide(x_ref[k])
        normed_ref[k] = low(x * rms_scale(x) * rows_ref[0:1, :])
        p = dot(normed_ref[k], w_ref[...], NT)
        out_ref[k] = low(p * cos_ref[...] + swap_halves(p) * sine_ref[...])


def head_columns(blocks_ref, head):
    per = blocks_ref.shape[2] // HEAD_DIM
    at = (head % per) * HEAD_DIM
    return blocks_ref[head // per, :, at : at + HEAD_DIM]


def attend_body(slots, len_ref, qkv_ref, prob_ref, att_ref):
    rows = qkv_ref.shape[1]
    seq_len = rows // slots
    shape = (GROUPS * rows, rows)
    row = lax.rem(lax.broadcasted_iota(jnp.int32, shape, 0), rows)
    col = lax.broadcasted_iota(jnp.int32, shape, 1)
    limit = jnp.zeros(shape, jnp.int32)
    for b in range(slots):
        limit = jnp.where(row >= b * seq_len, b * seq_len + len_ref[b], limit)
    first = row - lax.rem(row, seq_len)
    allowed = (col >= first) & (col <= row) & (col < limit)
    outs = []
    for g in range(KV_HEADS):
        q = jnp.concatenate([head_columns(qkv_ref, GROUPS * g + i) for i in range(GROUPS)], axis=0)
        k = head_columns(qkv_ref, HEADS + g)
        v = head_columns(qkv_ref, HEADS + KV_HEADS + g)
        s = jnp.where(allowed, dot(q, k, NT) * HEAD_DIM ** (-0.5), MASKED)
        e = jnp.exp(s - jnp.max(s, axis=-1, keepdims=True))
        p = e / jnp.sum(e, axis=-1, keepdims=True)
        prob_ref[g] = p
        o = dot(low(p), v, NN)
        outs += [o[i * rows : (i + 1) * rows] for i in range(GROUPS)]
    att_ref[...] = low(jnp.concatenate(outs, axis=1))


def out_body(n_z, at_ref, att_ref, x_ref, gain_ref, *refs):
    hidden_ref, normed_ref, wo_ref, sem = refs[-4:]
    parts = refs[:-4]
    copies = []
    if len(parts) == 1:
        copies.append(pltpu.make_async_copy(parts[0], wo_ref, sem))
    else:
        for c, part in enumerate(parts):
            for k in range(part.shape[0]):
                to = (at_ref[0] ^ (k // n_z)) * n_z + (at_ref[1] ^ (k % n_z))
                to = to * 2 + (at_ref[2] ^ c)
                copies.append(pltpu.make_async_copy(part.at[k], wo_ref.at[to], sem))
    for copy in copies:
        copy.start()
    for copy in copies:
        copy.wait()
    hidden = wide(x_ref[...]) + dot(att_ref[...], wo_ref[...].reshape(D, D), NT)
    hidden_ref[...] = hidden
    normed_ref[...] = low(hidden * rms_scale(hidden) * gain_ref[1:2, :])


def units_back_body(n, tile, *refs):
    dy_refs, (w_ref, rows_ref, out_ref, held_ref, sems) = refs[:n], refs[n:]
    tiles = range(0, held_ref.shape[0], tile)
    copies = [
        pltpu.make_async_copy(
            w_ref.at[2, pl.ds(j, tile)], held_ref.at[pl.ds(j, tile)], sems.at[i]
        )
        for i, j in enumerate(tiles)
    ]
    for copy in copies:
        copy.start()
    rows = dy_refs[0].shape[0]
    for k in range(n):
        rows_ref[k * rows : (k + 1) * rows, :] = dy_refs[k][...]
    for copy, j in zip(copies, tiles):
        copy.wait()
        out_ref[:, j : j + tile] = dot(rows_ref[...], held_ref[j : j + tile, :], NT)


def units_body(n, tile, *refs):
    n2_refs, (w_ref, da_ref) = refs[:n], refs[n : n + 2]
    rows_ref, act_ref, gate_ref, up_ref = refs[n + 2 : n + 6]
    own_ref, out_refs = refs[n + 6], refs[n + 7 : 2 * n + 6]
    held_ref, sems, row_sems = refs[2 * n + 6 :]
    tiles = range(0, held_ref.shape[1], tile)
    copies = [
        [
            pltpu.make_async_copy(
                w_ref.at[p, pl.ds(j, tile)], held_ref.at[p, pl.ds(j, tile)], sems.at[p, i]
            )
            for p in range(2)
        ]
        for i, j in enumerate(tiles)
    ]
    for pair in copies:
        for copy in pair:
            copy.start()
    rows = n2_refs[0].shape[0]
    moves = [
        pltpu.make_async_copy(n2_refs[k], rows_ref.at[pl.ds(k * rows, rows)], row_sems.at[k])
        for k in range(n)
    ]
    for move in moves:
        move.start()
    for move in moves:
        move.wait()
    for pair, j in zip(copies, tiles):
        for copy in pair:
            copy.wait()
        at = slice(j, j + tile)
        gate = dot(rows_ref[...], held_ref[0, at, :], NT)
        up = dot(rows_ref[...], held_ref[1, at, :], NT)
        da = da_ref[:, at]
        sig = jax.nn.sigmoid(gate)
        silu = gate * sig
        act_ref[:, at] = low(silu * up)
        gate_ref[:, at] = low(da * up * sig * (1.0 + gate * (1.0 - sig)))
        up_ref[:, at] = low(da * silu)
    for j in range(0, D, tile):
        at = slice(j, j + tile)
        back = dot(gate_ref[...], held_ref[0, :, at], NN) + dot(
            up_ref[...], held_ref[1, :, at], NN
        )
        own_ref[:, at] = back[:rows]
        for k in range(1, n):
            out_refs[k - 1][:, at] = low(back[k * rows : (k + 1) * rows])


def norm_back_body(n_z, n, at_ref, own_ref, *refs):
    got = refs[: n_z - 1]
    hidden_ref, gain_ref, up_ref = refs[n_z - 1 : n_z + 2]
    grad_ref, low_ref, gain_grad_ref = refs[n_z + 2 : n_z + 5]
    col_refs, held_ref, sems = refs[n_z + 5 : -2], refs[-2], refs[-1]
    width = D // n
    copies = [pltpu.make_async_copy(r, held_ref.at[k], sems.at[k]) for k, r in enumerate(got)]
    for copy in copies:
        copy.start()
    hidden = hidden_ref[...]
    scale = rms_scale(hidden)
    unit = hidden * scale
    dn = own_ref[...]
    for k, copy in enumerate(copies):
        copy.wait()
        dn = dn + wide(held_ref[k])
    gain_grad_ref[...] = jnp.sum(dn * unit, axis=0, keepdims=True)
    scaled = dn * gain_ref[1:2, :]
    grad = wide(up_ref[...]) + scale * (
        scaled - unit * jnp.mean(scaled * unit, axis=-1, keepdims=True)
    )
    grad_ref[...] = grad
    low_ref[...] = low(grad)
    if col_refs:
        for k in range(n):
            at = pl.multiple_of((at_ref[0] ^ k) * width, 128)
            col_refs[k][...] = low_ref[:, pl.ds(at, width)]


def attend_back_body(n, grad_ref, wo_ref, qkv_ref, prob_ref, cos_ref, sine_ref, heads_ref):
    rows = grad_ref.shape[0]
    do = low(dot(grad_ref[...], wo_ref[...], NN))
    grads = [None] * ALL_HEADS
    root = HEAD_DIM ** (-0.5)
    for g in range(KV_HEADS):
        q = jnp.concatenate([head_columns(qkv_ref, GROUPS * g + i) for i in range(GROUPS)], axis=0)
        k = head_columns(qkv_ref, HEADS + g)
        v = head_columns(qkv_ref, HEADS + KV_HEADS + g)
        d = jnp.concatenate(
            [
                do[:, h * HEAD_DIM : (h + 1) * HEAD_DIM]
                for h in range(GROUPS * g, GROUPS * g + GROUPS)
            ],
            axis=0,
        )
        p = prob_ref[g]
        dp = dot(d, v, NT)
        ds = low(p * (dp - jnp.sum(p * dp, axis=-1, keepdims=True)))
        dq = dot(ds, k, NN) * root
        for i in range(GROUPS):
            grads[GROUPS * g + i] = dq[i * rows : (i + 1) * rows]
        grads[HEADS + g] = dot(ds, q, TN) * root
        grads[HEADS + KV_HEADS + g] = dot(low(p), d, TN)
    per = ALL_HEADS // n
    for j in range(n):
        block = jnp.concatenate(grads[j * per : (j + 1) * per], axis=1)
        turned = max(0, min(per, HEADS + KV_HEADS - j * per))
        if turned:
            back = block * cos_ref[...] - swap_halves(block) * sine_ref[...]
            if turned < per:
                column = lax.broadcasted_iota(jnp.int32, block.shape, 1)
                back = jnp.where(column < turned * HEAD_DIM, back, block)
            block = back
        heads_ref[j] = low(block)


def units_grad_body(n, gate_ref, up_ref, act_ref, rows_ref, dy_ref, w_ref, *refs):
    out_ref, own_ref, part_refs = refs[0], refs[1], refs[2 : n + 1]
    held_ref, sem = refs[n + 1 :]
    copy = pltpu.make_async_copy(w_ref.at[2], held_ref, sem)
    copy.start()
    for j in range(0, gate_ref.shape[1], TILE):
        at = slice(j, j + TILE)
        out_ref[0, at, :] = low(dot(gate_ref[:, at], rows_ref[...], TN))
        out_ref[1, at, :] = low(dot(up_ref[:, at], rows_ref[...], TN))
        out_ref[2, at, :] = low(dot(act_ref[:, at], dy_ref[...], TN))
    copy.wait()
    rows = own_ref.shape[0]
    for j in range(0, D, TILE):
        at = slice(j, j + TILE)
        out = dot(act_ref[...], held_ref[:, at], NN)
        own_ref[:, at] = out[:rows]
        for k in range(1, n):
            part_refs[k - 1][:, at] = low(out[k * rows : (k + 1) * rows])


def columns_grad_body(n, at_ref, in_ref, normed_ref, att_ref, *refs):
    col_refs, (mine_ref, other_ref, held_ref, sum_ref) = refs[:n], refs[n:]
    for k in range(n):
        held_ref[at_ref[0] ^ k] = col_refs[k][...]
    n_z = mine_ref.shape[0]
    blocks = 2 * n_z
    grads = in_ref[...].reshape(-1, in_ref.shape[2])
    cols = held_ref[...].reshape(-1, held_ref.shape[2])
    normed = normed_ref[...].reshape(-1, D)
    att = att_ref[...].reshape(-1, D)
    first, second = grads.shape[1] // blocks, cols.shape[1] // blocks
    for j in range(0, D, 512):
        at = slice(j, j + 512)
        one = dot(grads, normed[:, at], TN)
        two = dot(cols, att[:, at], TN)
        for i in range(blocks):
            sum_ref[i, :first, at] = one[i * first : (i + 1) * first]
            sum_ref[i, first:, at] = two[i * second : (i + 1) * second]
    for z in range(n_z):
        i = (at_ref[1] ^ z) * 2
        mine_ref[z] = sum_ref[i + at_ref[2]]
        other_ref[z] = low(sum_ref[i + (at_ref[2] ^ 1)])


def add_body(mine_ref, other_ref, own_ref, *out_refs):
    own_ref[...] = mine_ref[0] + wide(other_ref[0])
    for k, ref in enumerate(out_refs):
        ref[...] = low(mine_ref[k + 1] + wide(other_ref[k + 1]))


def inputs_grad_body(grad_ref, w_ref, x_ref, out_ref, gain_ref):
    total = jnp.zeros((1, D), f32)
    for k in range(x_ref.shape[0]):
        back = dot(grad_ref[k], w_ref[...], NN)
        x = wide(x_ref[k])
        total = total + jnp.sum(back * (x * rms_scale(x)), axis=0, keepdims=True)
        out_ref[k] = low(back)
    gain_ref[...] = total


def settle_body(rate, n, *refs):
    grad_refs, refs = refs[:n], refs[n:]
    at = 0
    for ins, outs in ((refs[0:3], refs[6:11]), (refs[3:6], refs[11:16])):
        weight, moment, average = (r[...] for r in ins)
        gradient = sum(wide(r[at : at + weight.shape[0], :]) for r in grad_refs)
        at += weight.shape[0]
        for ref, value in zip(outs, update(weight, gradient, moment, average, rate)):
            ref[...] = value


def pack_body(gate_ref, down_ref, out_ref):
    out_ref[0] = low(gate_ref[0].T)
    out_ref[1] = low(gate_ref[1].T)
    out_ref[2] = low(down_ref[...])


def update_body(rate, flip, n, *refs):
    grad_ref, refs = refs[0], refs[1:]
    for i in range(n):
        weight, moment, average = (r[i] for r in refs[:3])
        gradient = wide(grad_ref[i].T if flip else grad_ref[i])
        for ref, value in zip(refs[3:], update(weight, gradient, moment, average, rate)):
            ref[i] = value


def update(weight, gradient, moment, average, step_rate):
    moment_new = MOMENTUM_RATE * moment + gradient
    weight_new = weight - step_rate * (gradient + MOMENTUM_RATE * moment_new)
    average_new = AVERAGE_RATE * average + (1.0 - AVERAGE_RATE) * weight_new
    return (gradient, moment_new, weight_new, average_new, weight_new.astype(bf16))


class Links:
    def __init__(self, n_dp, n_z):
        assert n_dp & (n_dp - 1) == 0 and n_z & (n_z - 1) == 0
        self.count = n_dp * n_z * 2
        self.dp = [n_z * 2 * k for k in range(n_dp)]
        self.z = [2 * k for k in range(n_z)]

    def send(self, values, mask):
        return lax.ppermute(values, AXES, [(i, i ^ mask) for i in range(self.count)])

    def gather(self, values, masks):
        return [values] + [self.send(values, m) for m in masks[1:]]

    def spread(self, blocks, masks):
        return [blocks[0]] + [self.send(b, m) for b, m in zip(blocks[1:], masks[1:])]


def block_of(values, index):
    return lax.dynamic_index_in_dim(values, index, keepdims=False)


def exchange(values, axes):
    return lax.all_to_all(values, axes, split_axis=0, concat_axis=0, tiled=True)


def tie(*values):
    return lax.optimization_barrier(values)


def on_device(
    tokens,
    cotangent,
    lengths,
    in_proj,
    out_proj,
    gate_up,
    down_proj,
    gains_pair,
    in_proj_mom,
    out_proj_mom,
    gate_up_mom,
    down_proj_mom,
    gains_mom,
    in_proj_avg,
    out_proj_avg,
    gate_up_avg,
    down_proj_avg,
    gains_avg,
):
    n_dp, n_z = lax.axis_size("dp"), lax.axis_size("z")
    n_zc = n_z * 2
    links = Links(n_dp, n_z)
    devices = links.count
    at_dp, at_z, at_core = (lax.axis_index(a) for a in AXES)
    at = jnp.stack([at_dp, at_z, at_core]).astype(jnp.int32)
    slots, seq_len = tokens.shape[:2]
    rows = slots * seq_len
    step_rate = RATE_BASE / math.sqrt(slots * devices * seq_len)
    in_width = in_proj.shape[1]
    out_width = out_proj.shape[1]
    ff_width = down_proj.shape[0]
    group = n_zc * in_width
    heads_here = group // HEAD_DIM
    aligned = in_width % 16 == 0 and out_width % 16 == 0

    in_low = low(jnp.transpose(in_proj))
    out_low = low(jnp.transpose(out_proj))
    gain_low = low(gains_pair)
    token_rows = tokens.reshape(rows, D)

    out_z = links.gather(out_low, links.z)
    in_group = lax.all_gather(in_low, ("z", "core"), axis=0, tiled=True)
    token_group = exchange(jnp.tile(token_rows[None], (n_dp, 1, 1)), "dp")
    cos_rows, sine_rows = rotary_rows(seq_len, slots, heads_here)
    head = at_dp * heads_here + jnp.arange(group) // HEAD_DIM
    turned = (head < HEADS + KV_HEADS)[None, :]
    cos_here = jnp.where(turned, cos_rows, 1.0)
    sine_here = jnp.where(turned, sine_rows, 0.0)
    gain_all = jnp.tile(gain_low.reshape(1, -1), (devices, 1))
    gain_all, cos_here, sine_here, cos_rows, sine_rows = tie(
        gain_all, cos_here, sine_here, cos_rows, sine_rows
    )
    gain_all, token_group, out_z = tie(gain_all, token_group, out_z)
    gain_all = exchange(gain_all, AXES)
    out_own = links.gather(jnp.stack(out_z), links.dp)
    gain_all, out_own, in_group = tie(gain_all, out_own, in_group)
    row_valid = (jnp.arange(seq_len)[None, :] < lengths[:, None]).reshape(rows, 1)
    upstream = jnp.where(row_valid, cotangent.reshape(rows, D), jnp.zeros((), bf16))
    upstream, in_group = tie(upstream, in_group)
    upstream_parts = links.gather(upstream, links.z)
    if not aligned:
        gain_all = wide(gain_all).reshape(devices, 2, -1)
        gain_all = jnp.swapaxes(gain_all, 0, 1).reshape(2, D)

    (ff_low,) = kernel_call(pack_body, [((3, ff_width, D), bf16)], [gate_up, down_proj])
    ff_low, in_group = tie(ff_low, in_group)
    ff = lax.all_gather(ff_low, PLANE, axis=1, tiled=True)

    blocks, normed_group, gain_rows = kernel_call(
        project_body,
        [
            ((n_dp, rows, group), bf16),
            ((n_dp, rows, D), bf16),
            ((2, D), f32),
        ],
        [token_group, in_group, gain_all, cos_here, sine_here],
    )
    qkv = exchange(blocks, "dp")

    out_own = jnp.stack(out_own).reshape(n_dp * n_z, out_width, D)
    out_other = links.send(out_own, 1)
    out_parts = [out_own, out_other]
    if not aligned:
        both = jnp.stack(out_parts)
        out_here = at_dp * n_z + at_z
        out_parts = [
            jnp.stack(
                [
                    block_of(block_of(both, at_core ^ c), out_here ^ k)
                    for k in range(n_dp * n_z)
                    for c in range(2)
                ]
            )
        ]

    prob, attended = kernel_call(
        functools.partial(attend_body, slots),
        [((KV_HEADS, GROUPS * rows, rows), f32), ((rows, D), bf16)],
        [lengths.astype(jnp.int32), qkv],
        smem=(0,),
    )
    attended, upstream_parts = tie(attended, upstream_parts)
    hidden, normed_two, out_full = kernel_call(
        functools.partial(out_body, n_z),
        [((rows, D), f32), ((rows, D), bf16), ((devices, out_width, D), bf16)],
        [at, attended, token_rows, gain_rows, *out_parts],
        smem=(0,),
        hbm=range(4, 4 + len(out_parts)),
        sems=[()],
    )
    out_full = out_full.reshape(D, D)

    normed_parts = links.gather(normed_two, links.z)
    attended_group = lax.all_gather(attended, "dp", axis=0)
    group_rows, units = n_z * rows, n_dp * 2 * ff_width
    upstream_group, grad_active = kernel_call(
        functools.partial(units_back_body, n_z, TILE),
        [((group_rows, D), bf16), ((group_rows, units), f32)],
        [*upstream_parts, ff],
        hbm=(n_z,),
        scratch=[((units, D), bf16)],
        sems=[(units // TILE,)],
    )
    normed_parts, grad_active = tie(normed_parts, grad_active)
    normed_rows, active, grad_gate, grad_up, *grad_normed = kernel_call(
        functools.partial(units_body, n_z, TILE),
        [((group_rows, D), bf16)]
        + [((group_rows, units), bf16)] * 3
        + [((rows, D), f32)]
        + [((rows, D), bf16)] * (n_z - 1),
        [*normed_parts, ff, grad_active],
        hbm=range(n_z + 1),
        scratch=[((2, units, D), bf16)],
        sems=[(2, units // TILE), (n_z,)],
    )
    grad_normed = links.spread(grad_normed, links.z)
    grad_ff, *partial_out = kernel_call(
        functools.partial(units_grad_body, n_z),
        [((3, units, D), bf16), ((rows, D), f32)] + [((rows, D), bf16)] * (n_z - 1),
        [grad_gate, grad_up, active, normed_rows, upstream_group, ff],
        hbm=(5,),
        scratch=[((units, D), bf16)],
        sems=[()],
    )
    grad_ff, partial_out, grad_normed = tie(grad_ff, partial_out, grad_normed)
    grad_ff = lax.psum_scatter(grad_ff, PLANE, scatter_dimension=1, tiled=True)
    partial_out = links.spread(partial_out, links.z)

    col_width = D // n_dp
    col_aligned = col_width % 128 == 0
    grad_hidden, grad_branch, gain_two_grad, *columns = kernel_call(
        functools.partial(norm_back_body, n_z, n_dp),
        [((rows, D), f32), ((rows, D), bf16), ((1, D), f32)]
        + ([((rows, col_width), bf16)] * n_dp if col_aligned else []),
        [at, *grad_normed, hidden, gain_rows, upstream],
        smem=(0,),
        hbm=range(2, n_z + 1),
        scratch=[((n_z - 1, rows, D), bf16)],
        sems=[(n_z - 1,)],
    )
    if not col_aligned:
        split = jnp.swapaxes(grad_branch.reshape(rows, n_dp, col_width), 0, 1)
        columns = [block_of(split, at_dp ^ k) for k in range(n_dp)]
    columns = links.spread(columns, links.dp)

    (blocks,) = kernel_call(
        functools.partial(attend_back_body, n_dp),
        [((n_dp, rows, group), bf16)],
        [grad_branch, out_full, qkv, prob, cos_rows, sine_rows],
    )
    blocks, partial_out[-1] = tie(blocks, partial_out[-1])
    grad_proj = exchange(blocks, "dp")
    grad_proj, partial_out, columns = tie(grad_proj, partial_out, columns)

    col_rows = in_width + out_width
    if aligned:
        mine, other = kernel_call(
            functools.partial(columns_grad_body, n_dp),
            [((n_z, col_rows, D), f32), ((n_z, col_rows, D), bf16)],
            [at, grad_proj, normed_group, attended_group, *columns],
            scratch=[((n_dp, rows, col_width), bf16), ((n_zc, col_rows, D), f32)],
            smem=(0,),
        )
    else:
        columns = jnp.stack(columns)
        columns = jnp.concatenate([block_of(columns, at_dp ^ k) for k in range(n_dp)])
        total = jnp.concatenate(
            [
                dot(lhs.reshape(n_dp * rows, -1), rhs.reshape(-1, D), TN).reshape(n_zc, -1, D)
                for lhs, rhs in ((grad_proj, normed_group), (columns, attended_group))
            ],
            axis=1,
        ).reshape(n_z, 2, col_rows, D)
        mine, other = (
            jnp.stack(
                [block_of(block_of(total, at_z ^ z), at_core ^ c) for z in range(n_z)]
            )
            for c in range(2)
        )
        other = low(other)
    grad_proj, mine = tie(grad_proj, mine)
    other = links.send(other, 1)
    grad_cols = kernel_call(
        add_body,
        [((col_rows, D), f32)] + [((col_rows, D), bf16)] * (n_z - 1),
        [mine, other],
    )
    grad_normed_one, gain_one_grad = kernel_call(
        inputs_grad_body,
        [((n_dp, rows, D), bf16), ((1, D), f32)],
        [grad_proj, in_group, token_group],
    )
    grad_gains = jnp.concatenate([gain_one_grad, gain_two_grad])
    grad_gains = jnp.swapaxes(grad_gains.reshape(2, devices, -1), 0, 1).reshape(devices, -1)
    grad_gains = exchange(grad_gains, AXES)
    grad_normed_one, grad_gains, grad_cols[0] = tie(grad_normed_one, grad_gains, grad_cols[0])
    grad_cols = links.spread(grad_cols, links.z)
    grad_gain = jnp.sum(grad_gains, axis=0).reshape(gains_pair.shape)
    parts = exchange(grad_normed_one, "dp")
    total_out = hidden + partial_out[0] + sum(wide(r) for r in partial_out[1:])
    produced = low(jnp.where(row_valid, total_out, 0.0))

    grad_normed_one = jnp.sum(wide(parts), axis=0)
    inputs = wide(token_rows)
    scale_one = rms_scale(inputs)
    unit_one = inputs * scale_one
    scaled_one = grad_normed_one * gain_rows[0:1]
    grad_inputs = grad_hidden + scale_one * (
        scaled_one - unit_one * jnp.mean(scaled_one * unit_one, axis=-1, keepdims=True)
    )


    def update_ff(grad, weight, moment, average, flip):
        outs = [(weight.shape, f32)] * 4 + [(weight.shape, bf16)]
        return kernel_call(
            functools.partial(update_body, step_rate, flip, weight.shape[0]),
            outs,
            [grad, weight, moment, average],
        )

    def settle(grads, *state):
        state = [jnp.transpose(v) for v in state]
        outs = kernel_call(
            functools.partial(settle_body, step_rate, len(grads)),
            [(v.shape, t) for v in state[::3] for t in (f32, f32, f32, f32, bf16)],
            [*grads, *state],
        )
        return [jnp.transpose(v) for v in outs]

    new_gate_up = update_ff(grad_ff[:2], gate_up, gate_up_mom, gate_up_avg, True)
    new_down = update(down_proj, wide(grad_ff[2]), down_proj_mom, down_proj_avg, step_rate)
    new_gains = update(gains_pair, grad_gain, gains_mom, gains_avg, step_rate)
    grad_cols, new_gate_up, new_down = tie(grad_cols, new_gate_up, new_down)
    new_cols = settle(
        grad_cols, in_proj, in_proj_mom, in_proj_avg, out_proj, out_proj_mom, out_proj_avg
    )
    return (
        produced.reshape(tokens.shape),
        grad_inputs.reshape(tokens.shape),
        *new_cols,
        *new_gate_up,
        *new_down,
        *new_gains,
    )


def solution(mesh):
    n_dp, n_fsdp = mesh.devices.shape
    fine = Mesh(mesh.devices.reshape(n_dp, n_fsdp // 2, 2), AXES)
    rows = P(AXES, None, None)
    last_of_two = P(None, AXES)
    first_of_two = P(AXES, None)
    last_of_three = P(None, None, AXES)
    weights = (last_of_two, last_of_two, last_of_three, first_of_two, last_of_two)
    in_specs = (rows, rows, P(AXES)) + weights * 3
    out_specs = (rows, rows) + tuple(spec for spec in weights for _ in range(5))
    return jax.shard_map(
        on_device, mesh=fine, in_specs=in_specs, out_specs=out_specs, check_vma=False
    )
```

```python
import functools
import math

import jax
import jax.numpy as jnp
from jax import lax
from jax.experimental import pallas as pl
from jax.experimental.pallas import tpu as pltpu
from jax.sharding import Mesh
from jax.sharding import PartitionSpec as P

D = 1536
HEADS = 16
KV_HEADS = 8
HEAD_DIM = 96
HALF = HEAD_DIM // 2
ALL_HEADS = HEADS + 2 * KV_HEADS
GROUPS = HEADS // KV_HEADS

EPS = 1e-05
THETA = 10000.0
MASKED = -1e30
MOMENTUM_RATE = 0.9
AVERAGE_RATE = 0.75
RATE_BASE = 0.1
AXES = ("dp", "z", "core")
PLANE = ("dp", "core")
NN = (((1,), (0,)), ((), ()))
TN = (((0,), (0,)), ((), ()))
NT = (((1,), (1,)), ((), ()))
VMEM_SLACK = 12 * 1024 * 1024
VMEM_ALL = 60 * 1024 * 1024
TILE = 256
SHORT = 30_000_000_000

bf16 = jnp.bfloat16
f32 = jnp.float32


def dot(a, b, dims):
    return lax.dot_general(a, b, dims, preferred_element_type=f32)


def low(values):
    return values.astype(bf16)


def wide(values):
    return values.astype(f32)


def rms_scale(values):
    return lax.rsqrt(jnp.mean(values * values, axis=-1, keepdims=True) + EPS)


def rotary_rows(seq_len, slots, heads):
    positions = jnp.arange(seq_len, dtype=f32)
    halves = jnp.arange(HALF, dtype=f32)
    frequencies = jnp.power(THETA, -2.0 * halves / HEAD_DIM)
    angles = positions[:, None] * frequencies[None, :]
    cos_table, sine_table = jnp.cos(angles), jnp.sin(angles)
    cos_rows = jnp.concatenate([cos_table, cos_table], axis=1)
    sine_rows = jnp.concatenate([-sine_table, sine_table], axis=1)
    return jnp.tile(cos_rows, (slots, heads)), jnp.tile(sine_rows, (slots, heads))


def swap_halves(values):
    width = values.shape[1]
    if width % 128 == 0:
        left = pltpu.roll(values, width - HALF, 1)
        right = pltpu.roll(values, HALF, 1)
    else:
        left = jnp.concatenate([values[:, HALF:], values[:, :HALF]], axis=1)
        right = jnp.concatenate([values[:, -HALF:], values[:, :-HALF]], axis=1)
    column = lax.broadcasted_iota(jnp.int32, values.shape, 1)
    return jnp.where(lax.rem(column, HEAD_DIM) < HALF, left, right)


def waited(copy, ref):
    copy.wait()
    return ref


def kernel_call(body, outs, ins, smem=(), hbm=(), late=(), scratch=(), sems=(), shared=False, flops=0):
    moved = [i for i in range(len(ins)) if i not in smem and i not in hbm]

    def fetched(*refs):
        given, rest = list(refs[: len(ins)]), refs[len(ins) :]
        held, sems = rest[-1 - len(moved) : -1], rest[-1]
        copies = [
            pltpu.make_async_copy(given[i], held[j], sems.at[j]) for j, i in enumerate(moved)
        ]
        for copy in copies:
            copy.start()
        for j, i in enumerate(moved):
            given[i] = held[j]
            if i in late:
                given[i] = functools.partial(waited, copies[j], held[j])
            else:
                copies[j].wait()
        body(*given, *rest[: -1 - len(moved)])

    arrays = [*outs, *((ins[i].shape, ins[i].dtype) for i in moved)]
    arrays += scratch
    held_bytes = sum(math.prod(s) * jnp.dtype(t).itemsize for s, t in arrays)
    outputs = pl.pallas_call(
        fetched,
        out_shape=[jax.ShapeDtypeStruct(s, t) for s, t in outs],
        in_specs=[
            pl.BlockSpec(memory_space=pltpu.SMEM if i in smem else pltpu.HBM)
            for i in range(len(ins))
        ],
        out_specs=[pl.BlockSpec(memory_space=pltpu.VMEM)] * len(outs),
        scratch_shapes=[
            *(pltpu.VMEM(s, t) for s, t in scratch),
            *(pltpu.SemaphoreType.DMA(s) for s in sems),
            *(pltpu.VMEM(ins[i].shape, ins[i].dtype) for i in moved),
            pltpu.SemaphoreType.DMA((len(moved),)),
        ],
        compiler_params=pltpu.CompilerParams(vmem_limit_bytes=held_bytes + VMEM_SLACK if shared else VMEM_ALL),
        cost_estimate=pl.CostEstimate(flops=flops, bytes_accessed=0, transcendentals=0),
    )(*ins)
    return list(outputs)


def project_body(at_ref, x_ref, w_ref, gains_ref, cos_ref, sine_ref, normed_ref, rows_ref, *refs):
    if gains_ref.shape[1] == D:
        rows_ref[...] = gains_ref[...]
    else:
        gains = wide(gains_ref[...])
        width = gains.shape[1] // 2
        for i in range(2):
            rows_ref[i : i + 1, :] = jnp.concatenate(
                [
                    gains[d : d + 1, i * width : (i + 1) * width]
                    for d in range(gains.shape[0])
                ],
                axis=1,
            )
    for k, ref in enumerate(refs):
        x = wide(x_ref[at_ref[0] ^ k])
        normed = low(x * rms_scale(x) * rows_ref[0:1, :])
        normed_ref[at_ref[0] ^ k] = normed
        p = dot(normed, w_ref[...], NT)
        ref[...] = low(p * cos_ref[...] + swap_halves(p) * sine_ref[...])


def head_columns(blocks_ref, head):
    per = blocks_ref.shape[2] // HEAD_DIM
    at = (head % per) * HEAD_DIM
    return blocks_ref[head // per, :, at : at + HEAD_DIM]


def attend_body(n, slots, at_ref, len_ref, *refs):
    in_refs, (qkv_ref, prob_ref, att_ref) = refs[:n], refs[n:]
    for k in range(n):
        qkv_ref[at_ref[0] ^ k] = in_refs[k][...]
    rows = qkv_ref.shape[1]
    seq_len = rows // slots
    shape = (GROUPS * rows, rows)
    row = lax.rem(lax.broadcasted_iota(jnp.int32, shape, 0), rows)
    col = lax.broadcasted_iota(jnp.int32, shape, 1)
    limit = jnp.zeros(shape, jnp.int32)
    for b in range(slots):
        limit = jnp.where(row >= b * seq_len, b * seq_len + len_ref[b], limit)
    first = row - lax.rem(row, seq_len)
    allowed = (col >= first) & (col <= row) & (col < limit)
    outs = []
    for g in range(KV_HEADS):
        q = jnp.concatenate([head_columns(qkv_ref, GROUPS * g + i) for i in range(GROUPS)], axis=0)
        k = head_columns(qkv_ref, HEADS + g)
        v = head_columns(qkv_ref, HEADS + KV_HEADS + g)
        s = jnp.where(allowed, dot(q, k, NT) * HEAD_DIM ** (-0.5), MASKED)
        e = jnp.exp(s - jnp.max(s, axis=-1, keepdims=True))
        p = e / jnp.sum(e, axis=-1, keepdims=True)
        prob_ref[g] = p
        o = dot(low(p), v, NN)
        outs += [o[i * rows : (i + 1) * rows] for i in range(GROUPS)]
    att_ref[...] = low(jnp.concatenate(outs, axis=1))


def out_body(n_z, at_ref, att_ref, x_ref, gain_ref, *refs):
    hidden_ref, normed_ref, wo_ref, sem = refs[-4:]
    parts = refs[:-4]
    copies = []
    if len(parts) == 1:
        copies.append(pltpu.make_async_copy(parts[0], wo_ref, sem))
    else:
        for c, part in enumerate(parts):
            for k in range(part.shape[0]):
                to = (at_ref[0] ^ (k // n_z)) * n_z + (at_ref[1] ^ (k % n_z))
                to = to * 2 + (at_ref[2] ^ c)
                copies.append(pltpu.make_async_copy(part.at[k], wo_ref.at[to], sem))
    for copy in copies:
        copy.start()
    for copy in copies:
        copy.wait()
    hidden = wide(x_ref[...]) + dot(att_ref[...], wo_ref[...].reshape(D, D), NT)
    hidden_ref[...] = hidden
    normed_ref[...] = low(hidden * rms_scale(hidden) * gain_ref[1:2, :])


def units_back_body(tile, at_ref, dy_ref, w_ref, rows_ref, out_ref, held_ref, sems):
    tiles = range(0, held_ref.shape[0], tile)
    copies = [
        pltpu.make_async_copy(
            w_ref.at[2, pl.ds(j, tile)], held_ref.at[pl.ds(j, tile)], sems.at[i]
        )
        for i, j in enumerate(tiles)
    ]
    for copy in copies:
        copy.start()
    rows = dy_ref.shape[1]
    for k in range(dy_ref.shape[0]):
        rows_ref[k * rows : (k + 1) * rows, :] = dy_ref[at_ref[1] ^ k]
    for copy, j in zip(copies, tiles):
        copy.wait()
        out_ref[:, j : j + tile] = dot(rows_ref[...], held_ref[j : j + tile, :], NT)


def units_body(n, tile, *refs):
    n2_refs, (w_ref, da_ref) = refs[:n], refs[n : n + 2]
    rows_ref, act_ref, gate_ref, up_ref = refs[n + 2 : n + 6]
    own_ref, out_refs = refs[n + 6], refs[n + 7 : 2 * n + 6]
    held_ref, sems, row_sems = refs[2 * n + 6 :]
    tiles = range(0, held_ref.shape[1], tile)
    copies = [
        [
            pltpu.make_async_copy(
                w_ref.at[p, pl.ds(j, tile)], held_ref.at[p, pl.ds(j, tile)], sems.at[p, i]
            )
            for p in range(2)
        ]
        for i, j in enumerate(tiles)
    ]
    for pair in copies:
        for copy in pair:
            copy.start()
    rows = n2_refs[0].shape[0]
    moves = [
        pltpu.make_async_copy(n2_refs[k], rows_ref.at[pl.ds(k * rows, rows)], row_sems.at[k])
        for k in range(n)
    ]
    for move in moves:
        move.start()
    for move in moves:
        move.wait()
    for pair, j in zip(copies, tiles):
        for copy in pair:
            copy.wait()
        at = slice(j, j + tile)
        gate = dot(rows_ref[...], held_ref[0, at, :], NT)
        up = dot(rows_ref[...], held_ref[1, at, :], NT)
        da = da_ref[:, at]
        sig = jax.nn.sigmoid(gate)
        silu = gate * sig
        act_ref[:, at] = low(silu * up)
        gate_ref[:, at] = low(da * up * sig * (1.0 + gate * (1.0 - sig)))
        up_ref[:, at] = low(da * silu)
    for j in range(0, D, tile):
        at = slice(j, j + tile)
        back = dot(gate_ref[...], held_ref[0, :, at], NN) + dot(
            up_ref[...], held_ref[1, :, at], NN
        )
        own_ref[:, at] = back[:rows]
        for k in range(1, n):
            out_refs[k - 1][:, at] = low(back[k * rows : (k + 1) * rows])


def attend_back_body(n, n_z, at_ref, own_ref, *refs):
    got = refs[: n_z - 1]
    hidden_ref, gain_ref, up_ref, late_wo, late_qkv, late_prob, late_cos, late_sine = refs[
        n_z - 1 : n_z + 7
    ]
    grad_ref, low_ref, gain_grad_ref, heads_ref = refs[n_z + 7 : n_z + 11]
    col_refs = refs[n_z + 11 :]
    hidden = hidden_ref[...]
    scale = rms_scale(hidden)
    unit = hidden * scale
    dn = own_ref[...]
    for late in got:
        dn = dn + wide(late()[...])
    gain_grad_ref[...] = jnp.sum(dn * unit, axis=0, keepdims=True)
    scaled = dn * gain_ref[1:2, :]
    grad = wide(up_ref[...]) + scale * (
        scaled - unit * jnp.mean(scaled * unit, axis=-1, keepdims=True)
    )
    grad_ref[...] = grad
    low_ref[...] = low(grad)
    width = D // n
    for k, ref in enumerate(col_refs):
        at = pl.multiple_of((at_ref[0] ^ k) * width, 128)
        ref[...] = low_ref[:, pl.ds(at, width)]

    wo_ref = late_wo()
    do = low(dot(low_ref[...], wo_ref[...], NN))
    qkv_ref, prob_ref, cos_ref, sine_ref = late_qkv(), late_prob(), late_cos(), late_sine()
    rows = do.shape[0]
    grads = [None] * ALL_HEADS
    root = HEAD_DIM ** (-0.5)
    for g in range(KV_HEADS):
        q = jnp.concatenate([head_columns(qkv_ref, GROUPS * g + i) for i in range(GROUPS)], axis=0)
        k = head_columns(qkv_ref, HEADS + g)
        v = head_columns(qkv_ref, HEADS + KV_HEADS + g)
        d = jnp.concatenate(
            [
                do[:, h * HEAD_DIM : (h + 1) * HEAD_DIM]
                for h in range(GROUPS * g, GROUPS * g + GROUPS)
            ],
            axis=0,
        )
        p = prob_ref[g]
        dp = dot(d, v, NT)
        ds = low(p * (dp - jnp.sum(p * dp, axis=-1, keepdims=True)))
        dq = dot(ds, k, NN) * root
        for i in range(GROUPS):
            grads[GROUPS * g + i] = dq[i * rows : (i + 1) * rows]
        grads[HEADS + g] = dot(ds, q, TN) * root
        grads[HEADS + KV_HEADS + g] = dot(low(p), d, TN)
    per = ALL_HEADS // n
    for j in range(n):
        block = jnp.concatenate(grads[j * per : (j + 1) * per], axis=1)
        turned = max(0, min(per, HEADS + KV_HEADS - j * per))
        if turned:
            back = block * cos_ref[...] - swap_halves(block) * sine_ref[...]
            if turned < per:
                column = lax.broadcasted_iota(jnp.int32, block.shape, 1)
                back = jnp.where(column < turned * HEAD_DIM, back, block)
            block = back
        heads_ref[j] = low(block)


def units_grad_body(n, gate_ref, up_ref, act_ref, rows_ref, dy_ref, w_ref, *refs):
    out_ref, own_ref, part_refs = refs[0], refs[1], refs[2 : n + 1]
    held_ref, sem = refs[n + 1 :]
    copy = pltpu.make_async_copy(w_ref.at[2], held_ref, sem)
    copy.start()
    for j in range(0, gate_ref.shape[1], TILE):
        at = slice(j, j + TILE)
        out_ref[0, at, :] = low(dot(gate_ref[:, at], rows_ref[...], TN))
        out_ref[1, at, :] = low(dot(up_ref[:, at], rows_ref[...], TN))
        out_ref[2, at, :] = low(dot(act_ref[:, at], dy_ref[...], TN))
    copy.wait()
    rows = own_ref.shape[0]
    for j in range(0, D, TILE):
        at = slice(j, j + TILE)
        out = dot(act_ref[...], held_ref[:, at], NN)
        own_ref[:, at] = out[:rows]
        for k in range(1, n):
            part_refs[k - 1][:, at] = low(out[k * rows : (k + 1) * rows])


def columns_grad_body(n, at_ref, late_in, late_normed, late_att, *refs):
    late_cols, (mine_ref, other_ref, held_ref, sum_ref) = refs[:n], refs[n:]
    n_z = mine_ref.shape[0]
    blocks = 2 * n_z
    in_ref, normed_ref = late_in(), late_normed()
    grads = in_ref[...].reshape(-1, in_ref.shape[2])
    normed = normed_ref[...].reshape(-1, D)
    first = grads.shape[1] // blocks
    for j in range(0, D, 512):
        at = slice(j, j + 512)
        one = dot(grads, normed[:, at], TN)
        for i in range(blocks):
            sum_ref[i, :first, at] = one[i * first : (i + 1) * first]
    for k in range(n):
        held_ref[at_ref[0] ^ k] = late_cols[k]()[...]
    cols = held_ref[...].reshape(-1, held_ref.shape[2])
    att = late_att()[...].reshape(-1, D)
    second = cols.shape[1] // blocks
    for j in range(0, D, 512):
        at = slice(j, j + 512)
        two = dot(cols, att[:, at], TN)
        for i in range(blocks):
            sum_ref[i, first:, at] = two[i * second : (i + 1) * second]
    for z in range(n_z):
        i = (at_ref[1] ^ z) * 2
        mine_ref[z] = sum_ref[i + at_ref[2]]
        other_ref[z] = low(sum_ref[i + (at_ref[2] ^ 1)])


def add_body(mine_ref, other_ref, own_ref, *out_refs):
    own_ref[...] = mine_ref[0] + wide(other_ref[0])
    for k, ref in enumerate(out_refs):
        ref[...] = low(mine_ref[k + 1] + wide(other_ref[k + 1]))


def inputs_grad_body(at_ref, grad_ref, w_ref, x_ref, second_ref, gain_ref, *out_refs):
    total = jnp.zeros((1, D), f32)
    for k, ref in enumerate(out_refs):
        back = dot(grad_ref[at_ref[0] ^ k], w_ref[...], NN)
        x = wide(x_ref[at_ref[0] ^ k])
        total = total + jnp.sum(back * (x * rms_scale(x)), axis=0, keepdims=True)
        ref[...] = back.astype(ref.dtype)
    if gain_ref.shape[1] == D:
        gain_ref[0:1, :] = total
        gain_ref[1:2, :] = second_ref[...]
    else:
        width = gain_ref.shape[1] // 2
        for d in range(gain_ref.shape[0]):
            at = slice(d * width, (d + 1) * width)
            gain_ref[d : d + 1, :width] = total[:, at]
            gain_ref[d : d + 1, width:] = second_ref[:, at]


def settle_body(rate, n, *refs):
    grad_refs, refs = refs[:n], refs[n:]
    at = 0
    for ins, outs in ((refs[0:3], refs[6:11]), (refs[3:6], refs[11:16])):
        weight, moment, average = (r[...] for r in ins)
        gradient = sum(wide(r[at : at + weight.shape[0], :]) for r in grad_refs)
        at += weight.shape[0]
        for ref, value in zip(outs, update(weight, gradient, moment, average, rate)):
            ref[...] = value


def pack_body(gate_ref, down_ref, out_ref):
    out_ref[0] = low(gate_ref[0].T)
    out_ref[1] = low(gate_ref[1].T)
    out_ref[2] = low(down_ref[...])


def update_body(rate, flip, n, *refs):
    grad_ref, refs = refs[0], refs[1:]
    for i in range(n):
        weight, moment, average = (r[i] for r in refs[:3])
        gradient = wide(grad_ref[i].T if flip else grad_ref[i])
        for ref, value in zip(refs[3:], update(weight, gradient, moment, average, rate)):
            ref[i] = value


def update(weight, gradient, moment, average, step_rate):
    moment_new = MOMENTUM_RATE * moment + gradient
    weight_new = weight - step_rate * (gradient + MOMENTUM_RATE * moment_new)
    average_new = AVERAGE_RATE * average + (1.0 - AVERAGE_RATE) * weight_new
    return (gradient, moment_new, weight_new, average_new, weight_new.astype(bf16))


class Links:
    def __init__(self, n_dp, n_z):
        assert n_dp & (n_dp - 1) == 0 and n_z & (n_z - 1) == 0
        self.count = n_dp * n_z * 2
        self.dp = [n_z * 2 * k for k in range(n_dp)]
        self.z = [2 * k for k in range(n_z)]

    def send(self, values, mask):
        return lax.ppermute(values, AXES, [(i, i ^ mask) for i in range(self.count)])

    def gather(self, values, masks):
        return [values] + [self.send(values, m) for m in masks[1:]]

    def spread(self, blocks, masks):
        return [blocks[0]] + [self.send(b, m) for b, m in zip(blocks[1:], masks[1:])]


def block_of(values, index):
    return lax.dynamic_index_in_dim(values, index, keepdims=False)


def exchange(values, axes):
    return lax.all_to_all(values, axes, split_axis=0, concat_axis=0, tiled=True)


def tie(*values):
    return lax.optimization_barrier(values)


def on_device(
    tokens,
    cotangent,
    lengths,
    in_proj,
    out_proj,
    gate_up,
    down_proj,
    gains_pair,
    in_proj_mom,
    out_proj_mom,
    gate_up_mom,
    down_proj_mom,
    gains_mom,
    in_proj_avg,
    out_proj_avg,
    gate_up_avg,
    down_proj_avg,
    gains_avg,
):
    n_dp, n_z = lax.axis_size("dp"), lax.axis_size("z")
    n_zc = n_z * 2
    links = Links(n_dp, n_z)
    devices = links.count
    at_dp, at_z, at_core = (lax.axis_index(a) for a in AXES)
    at = jnp.stack([at_dp, at_z, at_core]).astype(jnp.int32)
    slots, seq_len = tokens.shape[:2]
    rows = slots * seq_len
    step_rate = RATE_BASE / math.sqrt(slots * devices * seq_len)
    in_width = in_proj.shape[1]
    out_width = out_proj.shape[1]
    ff_width = down_proj.shape[0]
    group = n_zc * in_width
    heads_here = group // HEAD_DIM
    aligned = in_width % 16 == 0 and out_width % 16 == 0

    in_low = low(jnp.transpose(in_proj))
    out_low = low(jnp.transpose(out_proj))
    gain_low = low(gains_pair)
    token_rows = tokens.reshape(rows, D)

    out_z = links.gather(out_low, links.z)
    in_group = lax.all_gather(in_low, ("z", "core"), axis=0, tiled=True)
    token_group = exchange(jnp.tile(token_rows[None], (n_dp, 1, 1)), "dp")
    cos_rows, sine_rows = rotary_rows(seq_len, slots, heads_here)
    head = at_dp * heads_here + jnp.arange(group) // HEAD_DIM
    turned = (head < HEADS + KV_HEADS)[None, :]
    cos_here = jnp.where(turned, cos_rows, 1.0)
    sine_here = jnp.where(turned, sine_rows, 0.0)
    gain_all = jnp.tile(gain_low.reshape(1, -1), (devices, 1))
    gain_all, cos_here, sine_here, cos_rows, sine_rows = tie(
        gain_all, cos_here, sine_here, cos_rows, sine_rows
    )
    gain_all, token_group, out_z = tie(gain_all, token_group, out_z)
    gain_all = exchange(gain_all, AXES)
    out_own = links.gather(jnp.stack(out_z), links.dp)
    gain_all, out_own, in_group = tie(gain_all, out_own, in_group)
    row_valid = (jnp.arange(seq_len)[None, :] < lengths[:, None]).reshape(rows, 1)
    upstream = jnp.where(row_valid, cotangent.reshape(rows, D), jnp.zeros((), bf16))
    upstream_group, in_group = tie(jnp.tile(upstream[None], (n_z, 1, 1)), in_group)
    upstream_group = exchange(upstream_group, "z")
    if not aligned:
        gain_all = wide(gain_all).reshape(devices, 2, -1)
        gain_all = jnp.swapaxes(gain_all, 0, 1).reshape(2, D)

    (ff_low,) = kernel_call(pack_body, [((3, ff_width, D), bf16)], [gate_up, down_proj])
    ff_low, in_group = tie(ff_low, in_group)
    ff = lax.all_gather(ff_low, PLANE, axis=1, tiled=True)

    normed_group, gain_rows, *blocks = kernel_call(
        project_body,
        [((n_dp, rows, D), bf16), ((2, D), f32)] + [((rows, group), bf16)] * n_dp,
        [at, token_group, in_group, gain_all, cos_here, sine_here],
        smem=(0,),
    )
    blocks = links.spread(blocks, links.dp)
    normed_group, out_own = tie(normed_group, out_own)

    out_own = jnp.stack(out_own).reshape(n_dp * n_z, out_width, D)
    out_other = links.send(out_own, 1)
    out_parts = [out_own, out_other]
    if not aligned:
        both = jnp.stack(out_parts)
        out_here = at_dp * n_z + at_z
        out_parts = [
            jnp.stack(
                [
                    block_of(block_of(both, at_core ^ c), out_here ^ k)
                    for k in range(n_dp * n_z)
                    for c in range(2)
                ]
            )
        ]

    qkv, prob, attended = kernel_call(
        functools.partial(attend_body, n_dp, slots),
        [
            ((n_dp, rows, group), bf16),
            ((KV_HEADS, GROUPS * rows, rows), f32),
            ((rows, D), bf16),
        ],
        [at, lengths.astype(jnp.int32), *blocks],
        smem=(0, 1),
    )
    attended, upstream_group = tie(attended, upstream_group)
    hidden, normed_two, out_full = kernel_call(
        functools.partial(out_body, n_z),
        [((rows, D), f32), ((rows, D), bf16), ((devices, out_width, D), bf16)],
        [at, attended, token_rows, gain_rows, *out_parts],
        smem=(0,),
        hbm=range(4, 4 + len(out_parts)),
        sems=[()],
    )
    out_full = out_full.reshape(D, D)

    normed_parts = links.gather(normed_two, links.z)
    attended_group = lax.all_gather(attended, "dp", axis=0)
    group_rows, units = n_z * rows, n_dp * 2 * ff_width
    upstream_group, grad_active = kernel_call(
        functools.partial(units_back_body, TILE),
        [((group_rows, D), bf16), ((group_rows, units), f32)],
        [at, upstream_group, ff],
        smem=(0,),
        hbm=(2,),
        scratch=[((units, D), bf16)],
        sems=[(units // TILE,)],
        shared=True,
    )
    normed_parts, grad_active = tie(normed_parts, grad_active)
    normed_rows, active, grad_gate, grad_up, *grad_normed = kernel_call(
        functools.partial(units_body, n_z, TILE),
        [((group_rows, D), bf16)]
        + [((group_rows, units), bf16)] * 3
        + [((rows, D), f32)]
        + [((rows, D), bf16)] * (n_z - 1),
        [*normed_parts, ff, grad_active],
        hbm=range(n_z + 1),
        scratch=[((2, units, D), bf16)],
        sems=[(2, units // TILE), (n_z,)],
        shared=True,
    )
    grad_normed = links.spread(grad_normed, links.z)
    grad_ff, *partial_out = kernel_call(
        functools.partial(units_grad_body, n_z),
        [((3, units, D), bf16), ((rows, D), f32)] + [((rows, D), bf16)] * (n_z - 1),
        [grad_gate, grad_up, active, normed_rows, upstream_group, ff],
        hbm=(5,),
        scratch=[((units, D), bf16)],
        sems=[()],
        shared=True,
    )
    grad_ff = lax.psum_scatter(grad_ff, PLANE, scatter_dimension=1, tiled=True)
    partial_out, grad_normed = tie(partial_out, grad_normed)
    partial_out = links.spread(partial_out, links.z)

    col_width = D // n_dp
    col_aligned = col_width % 128 == 0
    grad_hidden, grad_branch, gain_two_grad, blocks, *columns = kernel_call(
        functools.partial(attend_back_body, n_dp, n_z),
        [((rows, D), f32), ((rows, D), bf16), ((1, D), f32), ((n_dp, rows, group), bf16)]
        + ([((rows, col_width), bf16)] * n_dp if col_aligned else []),
        [
            at,
            *grad_normed,
            hidden,
            gain_rows,
            upstream,
            out_full,
            qkv,
            prob,
            cos_rows,
            sine_rows,
        ],
        smem=(0,),
        late=(*range(2, n_z + 1), *range(n_z + 4, n_z + 9)),
        flops=SHORT,
    )
    if not col_aligned:
        split = jnp.swapaxes(grad_branch.reshape(rows, n_dp, col_width), 0, 1)
        columns = [block_of(split, at_dp ^ k) for k in range(n_dp)]
    columns = links.spread(columns, links.dp)

    blocks, partial_out[-1] = tie(blocks, partial_out[-1])
    grad_proj = exchange(blocks, "dp")
    grad_proj, columns = tie(grad_proj, columns)

    col_rows = in_width + out_width

    if aligned:
        mine, other = kernel_call(
            functools.partial(columns_grad_body, n_dp),
            [((n_z, col_rows, D), f32), ((n_z, col_rows, D), bf16)],
            [at, grad_proj, normed_group, attended_group, *columns],
            scratch=[((n_dp, rows, col_width), bf16), ((n_zc, col_rows, D), f32)],
            smem=(0,),
            late=range(1, n_dp + 4),
            flops=SHORT,
        )
    else:
        columns = jnp.stack(columns)
        columns = jnp.concatenate([block_of(columns, at_dp ^ k) for k in range(n_dp)])
        total = jnp.concatenate(
            [
                dot(lhs.reshape(n_dp * rows, -1), rhs.reshape(-1, D), TN).reshape(n_zc, -1, D)
                for lhs, rhs in ((grad_proj, normed_group), (columns, attended_group))
            ],
            axis=1,
        ).reshape(n_z, 2, col_rows, D)
        mine, other = (
            jnp.stack([block_of(block_of(total, at_z ^ z), at_core ^ c) for z in range(n_z)])
            for c in range(2)
        )
        other = low(other)
    grad_proj, mine = tie(grad_proj, mine)
    other = links.send(other, 1)
    grad_gains, *grad_normed_one = kernel_call(
        inputs_grad_body,
        [((devices, D // devices * 2) if aligned else (2, D), f32), ((rows, D), f32)]
        + [((rows, D), bf16)] * (n_dp - 1),
        [at, grad_proj, in_group, token_group, gain_two_grad],
        smem=(0,),
        flops=SHORT,
    )
    if not aligned:
        grad_gains = jnp.swapaxes(grad_gains.reshape(2, devices, -1), 0, 1).reshape(devices, -1)
    other, partial_out = tie(other, partial_out)
    grad_cols = kernel_call(
        add_body,
        [((col_rows, D), f32)] + [((col_rows, D), bf16)] * (n_z - 1),
        [mine, other],
    )
    grad_normed_one, grad_gains, grad_cols[0] = tie(grad_normed_one, grad_gains, grad_cols[0])
    grad_cols = links.spread(grad_cols, links.z)
    parts = [grad_normed_one[0]]
    for k in range(1, n_dp):
        parts.append(links.send(grad_normed_one[k], links.dp[k]))
    grad_gains = exchange(grad_gains, AXES)
    total_out = hidden + partial_out[0] + sum(wide(r) for r in partial_out[1:])
    produced = low(jnp.where(row_valid, total_out, 0.0))

    grad_normed_one = parts[0] + sum(wide(r) for r in parts[1:])
    inputs = wide(token_rows)
    scale_one = rms_scale(inputs)
    unit_one = inputs * scale_one
    scaled_one = grad_normed_one * gain_rows[0:1]
    grad_inputs = grad_hidden + scale_one * (
        scaled_one - unit_one * jnp.mean(scaled_one * unit_one, axis=-1, keepdims=True)
    )


    def update_ff(grad, weight, moment, average, flip):
        outs = [(weight.shape, f32)] * 4 + [(weight.shape, bf16)]
        return kernel_call(
            functools.partial(update_body, step_rate, flip, weight.shape[0]),
            outs,
            [grad, weight, moment, average],
        )

    def settle(grads, *state):
        state = [jnp.transpose(v) for v in state]
        outs = kernel_call(
            functools.partial(settle_body, step_rate, len(grads)),
            [(v.shape, t) for v in state[::3] for t in (f32, f32, f32, f32, bf16)],
            [*grads, *state],
        )
        return [jnp.transpose(v) for v in outs]

    new_gate_up = update_ff(grad_ff[:2], gate_up, gate_up_mom, gate_up_avg, True)
    new_down = update(down_proj, wide(grad_ff[2]), down_proj_mom, down_proj_avg, step_rate)
    grad_cols, grad_gains, new_gate_up, new_down = tie(
        grad_cols, grad_gains, new_gate_up, new_down
    )
    grad_gain = jnp.sum(grad_gains, axis=0).reshape(gains_pair.shape)
    new_gains = update(gains_pair, grad_gain, gains_mom, gains_avg, step_rate)
    new_cols = settle(
        grad_cols, in_proj, in_proj_mom, in_proj_avg, out_proj, out_proj_mom, out_proj_avg
    )
    return (
        produced.reshape(tokens.shape),
        grad_inputs.reshape(tokens.shape),
        *new_cols,
        *new_gate_up,
        *new_down,
        *new_gains,
    )


def solution(mesh):
    n_dp, n_fsdp = mesh.devices.shape
    fine = Mesh(mesh.devices.reshape(n_dp, n_fsdp // 2, 2), AXES)
    rows = P(AXES, None, None)
    last_of_two = P(None, AXES)
    first_of_two = P(AXES, None)
    last_of_three = P(None, None, AXES)
    weights = (last_of_two, last_of_two, last_of_three, first_of_two, last_of_two)
    in_specs = (rows, rows, P(AXES)) + weights * 3
    out_specs = (rows, rows) + tuple(spec for spec in weights for _ in range(5))
    return jax.shard_map(
        on_device, mesh=fine, in_specs=in_specs, out_specs=out_specs, check_vma=False
    )
```

```python
import functools
import math

import jax
import jax.numpy as jnp
from jax import lax
from jax.experimental import pallas as pl
from jax.experimental.pallas import tpu as pltpu
from jax.sharding import Mesh
from jax.sharding import PartitionSpec as P

D = 1536
HEADS = 16
KV_HEADS = 8
HEAD_DIM = 96
HALF = HEAD_DIM // 2
ALL_HEADS = HEADS + 2 * KV_HEADS
GROUPS = HEADS // KV_HEADS

EPS = 1e-05
THETA = 10000.0
MASKED = -1e30
MOMENTUM_RATE = 0.9
AVERAGE_RATE = 0.75
RATE_BASE = 0.1
AXES = ("dp", "z", "core")
PLANE = ("dp", "core")
NN = (((1,), (0,)), ((), ()))
TN = (((0,), (0,)), ((), ()))
NT = (((1,), (1,)), ((), ()))
VMEM_SLACK = 12 * 1024 * 1024
VMEM_ALL = 60 * 1024 * 1024
TILE = 256
SHORT = 30_000_000_000
LONG = 300_000_000_000

bf16 = jnp.bfloat16
f32 = jnp.float32


def dot(a, b, dims):
    return lax.dot_general(a, b, dims, preferred_element_type=f32)


def low(values):
    return values.astype(bf16)


def wide(values):
    return values.astype(f32)


def rms_scale(values):
    return lax.rsqrt(jnp.mean(values * values, axis=-1, keepdims=True) + EPS)


def rotary_rows(seq_len, slots, heads):
    positions = jnp.arange(seq_len, dtype=f32)
    halves = jnp.arange(HALF, dtype=f32)
    frequencies = jnp.power(THETA, -2.0 * halves / HEAD_DIM)
    angles = positions[:, None] * frequencies[None, :]
    cos_table, sine_table = jnp.cos(angles), jnp.sin(angles)
    cos_rows = jnp.concatenate([cos_table, cos_table], axis=1)
    sine_rows = jnp.concatenate([-sine_table, sine_table], axis=1)
    return jnp.tile(cos_rows, (slots, heads)), jnp.tile(sine_rows, (slots, heads))


def swap_halves(values):
    width = values.shape[1]
    if width % 128 == 0:
        left = pltpu.roll(values, width - HALF, 1)
        right = pltpu.roll(values, HALF, 1)
    else:
        left = jnp.concatenate([values[:, HALF:], values[:, :HALF]], axis=1)
        right = jnp.concatenate([values[:, -HALF:], values[:, :-HALF]], axis=1)
    column = lax.broadcasted_iota(jnp.int32, values.shape, 1)
    return jnp.where(lax.rem(column, HEAD_DIM) < HALF, left, right)


def waited(copy, ref):
    copy.wait()
    return ref


def kernel_call(
    body, outs, ins, smem=(), hbm=(), late=(), far=(), scratch=(), sems=(), shared=False, flops=0
):
    moved = [i for i in range(len(ins)) if i not in smem and i not in hbm]

    def fetched(*refs):
        given, rest = list(refs[: len(ins)]), refs[len(ins) :]
        held, sems = rest[-1 - len(moved) : -1], rest[-1]
        copies = [
            pltpu.make_async_copy(given[i], held[j], sems.at[j]) for j, i in enumerate(moved)
        ]
        for copy in copies:
            copy.start()
        for j, i in enumerate(moved):
            given[i] = held[j]
            if i in late:
                given[i] = functools.partial(waited, copies[j], held[j])
            else:
                copies[j].wait()
        body(*given, *rest[: -1 - len(moved)])

    arrays = [v for i, v in enumerate(outs) if i not in far]
    arrays += [*((ins[i].shape, ins[i].dtype) for i in moved)]
    arrays += scratch
    held_bytes = sum(math.prod(s) * jnp.dtype(t).itemsize for s, t in arrays)
    outputs = pl.pallas_call(
        fetched,
        out_shape=[jax.ShapeDtypeStruct(s, t) for s, t in outs],
        in_specs=[
            pl.BlockSpec(memory_space=pltpu.SMEM if i in smem else pltpu.HBM)
            for i in range(len(ins))
        ],
        out_specs=[
            pl.BlockSpec(memory_space=pltpu.HBM if i in far else pltpu.VMEM)
            for i in range(len(outs))
        ],
        scratch_shapes=[
            *(pltpu.VMEM(s, t) for s, t in scratch),
            *(pltpu.SemaphoreType.DMA(s) for s in sems),
            *(pltpu.VMEM(ins[i].shape, ins[i].dtype) for i in moved),
            pltpu.SemaphoreType.DMA((len(moved),)),
        ],
        compiler_params=pltpu.CompilerParams(vmem_limit_bytes=held_bytes + VMEM_SLACK if shared else VMEM_ALL),
        cost_estimate=pl.CostEstimate(flops=flops, bytes_accessed=0, transcendentals=0),
    )(*ins)
    return list(outputs)


def project_body(at_ref, x_ref, w_ref, gains_ref, cos_ref, sine_ref, normed_ref, rows_ref, *refs):
    if gains_ref.shape[1] == D:
        rows_ref[...] = gains_ref[...]
    else:
        gains = wide(gains_ref[...])
        width = gains.shape[1] // 2
        for i in range(2):
            rows_ref[i : i + 1, :] = jnp.concatenate(
                [
                    gains[d : d + 1, i * width : (i + 1) * width]
                    for d in range(gains.shape[0])
                ],
                axis=1,
            )
    for k, ref in enumerate(refs):
        x = wide(x_ref[at_ref[0] ^ k])
        normed = low(x * rms_scale(x) * rows_ref[0:1, :])
        normed_ref[at_ref[0] ^ k] = normed
        p = dot(normed, w_ref[...], NT)
        ref[...] = low(p * cos_ref[...] + swap_halves(p) * sine_ref[...])


def head_columns(blocks_ref, head):
    per = blocks_ref.shape[2] // HEAD_DIM
    at = (head % per) * HEAD_DIM
    return blocks_ref[head // per, :, at : at + HEAD_DIM]


def attend_body(n, slots, at_ref, len_ref, *refs):
    in_refs, (qkv_ref, prob_ref, att_ref) = refs[:n], refs[n:]
    for k in range(n):
        qkv_ref[at_ref[0] ^ k] = in_refs[k][...]
    rows = qkv_ref.shape[1]
    seq_len = rows // slots
    shape = (GROUPS * rows, rows)
    row = lax.rem(lax.broadcasted_iota(jnp.int32, shape, 0), rows)
    col = lax.broadcasted_iota(jnp.int32, shape, 1)
    limit = jnp.zeros(shape, jnp.int32)
    for b in range(slots):
        limit = jnp.where(row >= b * seq_len, b * seq_len + len_ref[b], limit)
    first = row - lax.rem(row, seq_len)
    allowed = (col >= first) & (col <= row) & (col < limit)
    outs = []
    for g in range(KV_HEADS):
        q = jnp.concatenate([head_columns(qkv_ref, GROUPS * g + i) for i in range(GROUPS)], axis=0)
        k = head_columns(qkv_ref, HEADS + g)
        v = head_columns(qkv_ref, HEADS + KV_HEADS + g)
        s = jnp.where(allowed, dot(q, k, NT) * HEAD_DIM ** (-0.5), MASKED)
        e = jnp.exp(s - jnp.max(s, axis=-1, keepdims=True))
        p = e / jnp.sum(e, axis=-1, keepdims=True)
        prob_ref[g] = p
        o = dot(low(p), v, NN)
        outs += [o[i * rows : (i + 1) * rows] for i in range(GROUPS)]
    att_ref[...] = low(jnp.concatenate(outs, axis=1))


def place_copies(n_z, at_ref, parts, wo_ref, sem):
    if len(parts) == 1:
        return [pltpu.make_async_copy(parts[0], wo_ref, sem)]
    copies = []
    for c, part in enumerate(parts):
        for k in range(part.shape[0]):
            to = (at_ref[0] ^ (k // n_z)) * n_z + (at_ref[1] ^ (k % n_z))
            to = to * 2 + (at_ref[2] ^ c)
            copies.append(pltpu.make_async_copy(part.at[k], wo_ref.at[to], sem))
    return copies


def place_body(n_z, at_ref, *refs):
    copies = place_copies(n_z, at_ref, refs[:-2], refs[-2], refs[-1])
    for copy in copies:
        copy.start()
    for copy in copies:
        copy.wait()


def out_body(n_z, at_ref, att_ref, x_ref, gain_ref, *refs):
    parts, (hidden_ref, normed_ref, wo_ref, sem) = refs[:-4], refs[-4:]
    copies = place_copies(n_z, at_ref, parts, wo_ref, sem)
    for copy in copies:
        copy.start()
    for copy in copies:
        copy.wait()
    hidden = wide(x_ref[...]) + dot(att_ref[...], wo_ref[...].reshape(D, D), NT)
    hidden_ref[...] = hidden
    normed_ref[...] = low(hidden * rms_scale(hidden) * gain_ref[1:2, :])


def units_back_body(tile, at_ref, dy_ref, w_ref, rows_ref, out_ref, held_ref, sems):
    tiles = range(0, held_ref.shape[0], tile)
    copies = [
        pltpu.make_async_copy(
            w_ref.at[2, pl.ds(j, tile)], held_ref.at[pl.ds(j, tile)], sems.at[i]
        )
        for i, j in enumerate(tiles)
    ]
    for copy in copies:
        copy.start()
    rows = dy_ref.shape[1]
    for k in range(dy_ref.shape[0]):
        rows_ref[k * rows : (k + 1) * rows, :] = dy_ref[at_ref[1] ^ k]
    for copy, j in zip(copies, tiles):
        copy.wait()
        out_ref[:, j : j + tile] = dot(rows_ref[...], held_ref[j : j + tile, :], NT)


def units_body(n, tile, *refs):
    n2_refs, (w_ref, da_ref) = refs[:n], refs[n : n + 2]
    rows_ref, act_ref, gate_ref, up_ref = refs[n + 2 : n + 6]
    own_ref, out_refs = refs[n + 6], refs[n + 7 : 2 * n + 6]
    held_ref, sems, row_sems = refs[2 * n + 6 :]
    tiles = range(0, held_ref.shape[1], tile)
    copies = [
        [
            pltpu.make_async_copy(
                w_ref.at[p, pl.ds(j, tile)], held_ref.at[p, pl.ds(j, tile)], sems.at[p, i]
            )
            for p in range(2)
        ]
        for i, j in enumerate(tiles)
    ]
    for pair in copies:
        for copy in pair:
            copy.start()
    rows = n2_refs[0].shape[0]
    moves = [
        pltpu.make_async_copy(n2_refs[k], rows_ref.at[pl.ds(k * rows, rows)], row_sems.at[k])
        for k in range(n)
    ]
    for move in moves:
        move.start()
    for move in moves:
        move.wait()
    for pair, j in zip(copies, tiles):
        for copy in pair:
            copy.wait()
        at = slice(j, j + tile)
        gate = dot(rows_ref[...], held_ref[0, at, :], NT)
        up = dot(rows_ref[...], held_ref[1, at, :], NT)
        da = da_ref[:, at]
        sig = jax.nn.sigmoid(gate)
        silu = gate * sig
        act_ref[:, at] = low(silu * up)
        gate_ref[:, at] = low(da * up * sig * (1.0 + gate * (1.0 - sig)))
        up_ref[:, at] = low(da * silu)
    for j in range(0, D, tile):
        at = slice(j, j + tile)
        back = dot(gate_ref[...], held_ref[0, :, at], NN) + dot(
            up_ref[...], held_ref[1, :, at], NN
        )
        own_ref[:, at] = back[:rows]
        for k in range(1, n):
            out_refs[k - 1][:, at] = low(back[k * rows : (k + 1) * rows])


def attend_back_body(n, n_z, at_ref, own_ref, *refs):
    got = refs[: n_z - 1]
    hidden_ref, gain_ref, up_ref, late_wo, late_qkv, late_prob, late_cos, late_sine = refs[
        n_z - 1 : n_z + 7
    ]
    grad_ref, low_ref, gain_grad_ref, heads_ref = refs[n_z + 7 : n_z + 11]
    col_refs = refs[n_z + 11 :]
    hidden = hidden_ref[...]
    scale = rms_scale(hidden)
    unit = hidden * scale
    dn = own_ref[...]
    for late in got:
        dn = dn + wide(late()[...])
    gain_grad_ref[...] = jnp.sum(dn * unit, axis=0, keepdims=True)
    scaled = dn * gain_ref[1:2, :]
    grad = wide(up_ref[...]) + scale * (
        scaled - unit * jnp.mean(scaled * unit, axis=-1, keepdims=True)
    )
    grad_ref[...] = grad
    low_ref[...] = low(grad)
    width = D // n
    for k, ref in enumerate(col_refs):
        at = pl.multiple_of((at_ref[0] ^ k) * width, 128)
        ref[...] = low_ref[:, pl.ds(at, width)]

    wo_ref = late_wo()
    do = low(dot(low_ref[...], wo_ref[...], NN))
    qkv_ref, prob_ref, cos_ref, sine_ref = late_qkv(), late_prob(), late_cos(), late_sine()
    rows = do.shape[0]
    grads = [None] * ALL_HEADS
    root = HEAD_DIM ** (-0.5)
    for g in range(KV_HEADS):
        q = jnp.concatenate([head_columns(qkv_ref, GROUPS * g + i) for i in range(GROUPS)], axis=0)
        k = head_columns(qkv_ref, HEADS + g)
        v = head_columns(qkv_ref, HEADS + KV_HEADS + g)
        d = jnp.concatenate(
            [
                do[:, h * HEAD_DIM : (h + 1) * HEAD_DIM]
                for h in range(GROUPS * g, GROUPS * g + GROUPS)
            ],
            axis=0,
        )
        p = prob_ref[g]
        dp = dot(d, v, NT)
        ds = low(p * (dp - jnp.sum(p * dp, axis=-1, keepdims=True)))
        dq = dot(ds, k, NN) * root
        for i in range(GROUPS):
            grads[GROUPS * g + i] = dq[i * rows : (i + 1) * rows]
        grads[HEADS + g] = dot(ds, q, TN) * root
        grads[HEADS + KV_HEADS + g] = dot(low(p), d, TN)
    per = ALL_HEADS // n
    for j in range(n):
        block = jnp.concatenate(grads[j * per : (j + 1) * per], axis=1)
        turned = max(0, min(per, HEADS + KV_HEADS - j * per))
        if turned:
            back = block * cos_ref[...] - swap_halves(block) * sine_ref[...]
            if turned < per:
                column = lax.broadcasted_iota(jnp.int32, block.shape, 1)
                back = jnp.where(column < turned * HEAD_DIM, back, block)
            block = back
        heads_ref[j] = low(block)


def units_grad_body(n, gate_ref, up_ref, act_ref, rows_ref, dy_ref, w_ref, *refs):
    out_ref, own_ref, part_refs = refs[0], refs[1], refs[2 : n + 1]
    held_ref, sem = refs[n + 1 :]
    copy = pltpu.make_async_copy(w_ref.at[2], held_ref, sem)
    copy.start()
    for j in range(0, gate_ref.shape[1], TILE):
        at = slice(j, j + TILE)
        out_ref[0, at, :] = low(dot(gate_ref[:, at], rows_ref[...], TN))
        out_ref[1, at, :] = low(dot(up_ref[:, at], rows_ref[...], TN))
        out_ref[2, at, :] = low(dot(act_ref[:, at], dy_ref[...], TN))
    copy.wait()
    rows = own_ref.shape[0]
    for j in range(0, D, TILE):
        at = slice(j, j + TILE)
        out = dot(act_ref[...], held_ref[:, at], NN)
        own_ref[:, at] = out[:rows]
        for k in range(1, n):
            part_refs[k - 1][:, at] = low(out[k * rows : (k + 1) * rows])


def columns_grad_body(n, at_ref, late_in, late_normed, late_att, *refs):
    late_cols, (mine_ref, other_ref, held_ref, sum_ref) = refs[:n], refs[n:]
    n_z = mine_ref.shape[0]
    blocks = 2 * n_z
    in_ref, normed_ref = late_in(), late_normed()
    grads = in_ref[...].reshape(-1, in_ref.shape[2])
    normed = normed_ref[...].reshape(-1, D)
    first = grads.shape[1] // blocks
    for j in range(0, D, 512):
        at = slice(j, j + 512)
        one = dot(grads, normed[:, at], TN)
        for i in range(blocks):
            sum_ref[i, :first, at] = one[i * first : (i + 1) * first]
    for k in range(n):
        held_ref[at_ref[0] ^ k] = late_cols[k]()[...]
    cols = held_ref[...].reshape(-1, held_ref.shape[2])
    att = late_att()[...].reshape(-1, D)
    second = cols.shape[1] // blocks
    for j in range(0, D, 512):
        at = slice(j, j + 512)
        two = dot(cols, att[:, at], TN)
        for i in range(blocks):
            sum_ref[i, first:, at] = two[i * second : (i + 1) * second]
    for z in range(n_z):
        i = (at_ref[1] ^ z) * 2
        mine_ref[z] = sum_ref[i + at_ref[2]]
        other_ref[z] = low(sum_ref[i + (at_ref[2] ^ 1)])


def add_body(mine_ref, other_ref, own_ref, *out_refs):
    own_ref[...] = mine_ref[0] + wide(other_ref[0])
    for k, ref in enumerate(out_refs):
        ref[...] = low(mine_ref[k + 1] + wide(other_ref[k + 1]))


def inputs_grad_body(at_ref, grad_ref, w_ref, x_ref, second_ref, gain_ref, *out_refs):
    total = jnp.zeros((1, D), f32)
    for k, ref in enumerate(out_refs):
        back = dot(grad_ref[at_ref[0] ^ k], w_ref[...], NN)
        x = wide(x_ref[at_ref[0] ^ k])
        total = total + jnp.sum(back * (x * rms_scale(x)), axis=0, keepdims=True)
        ref[...] = back.astype(ref.dtype)
    if gain_ref.shape[1] == D:
        gain_ref[0:1, :] = total
        gain_ref[1:2, :] = second_ref[...]
    else:
        width = gain_ref.shape[1] // 2
        for d in range(gain_ref.shape[0]):
            at = slice(d * width, (d + 1) * width)
            gain_ref[d : d + 1, :width] = total[:, at]
            gain_ref[d : d + 1, width:] = second_ref[:, at]


def settle_body(rate, n, *refs):
    grad_refs, refs = refs[:n], refs[n:]
    at = 0
    for ins, outs in ((refs[0:3], refs[6:11]), (refs[3:6], refs[11:16])):
        weight, moment, average = (r[...] for r in ins)
        gradient = sum(wide(r[at : at + weight.shape[0], :]) for r in grad_refs)
        at += weight.shape[0]
        for ref, value in zip(outs, update(weight, gradient, moment, average, rate)):
            ref[...] = value


def pack_body(gate_ref, down_ref, up_ref, out_ref, copies_ref):
    for k in range(copies_ref.shape[0]):
        copies_ref[k] = up_ref[...]
    out_ref[0] = low(gate_ref[0].T)
    out_ref[1] = low(gate_ref[1].T)
    out_ref[2] = low(down_ref[...])


def update_body(rate, grad_ref, *refs):
    ins, outs = refs[:6], refs[6:]
    for p in range(2):
        weight, moment, average = (r[p] for r in ins[:3])
        gradient = wide(grad_ref[p].T)
        for ref, value in zip(outs[:5], update(weight, gradient, moment, average, rate)):
            ref[p] = value
    weight, moment, average = (r[...] for r in ins[3:])
    for ref, value in zip(outs[5:], update(weight, wide(grad_ref[2]), moment, average, rate)):
        ref[...] = value


def update(weight, gradient, moment, average, step_rate):
    moment_new = MOMENTUM_RATE * moment + gradient
    weight_new = weight - step_rate * (gradient + MOMENTUM_RATE * moment_new)
    average_new = AVERAGE_RATE * average + (1.0 - AVERAGE_RATE) * weight_new
    return (gradient, moment_new, weight_new, average_new, weight_new.astype(bf16))


class Links:
    def __init__(self, n_dp, n_z):
        assert n_dp & (n_dp - 1) == 0 and n_z & (n_z - 1) == 0
        self.count = n_dp * n_z * 2
        self.dp = [n_z * 2 * k for k in range(n_dp)]
        self.z = [2 * k for k in range(n_z)]

    def send(self, values, mask):
        return lax.ppermute(values, AXES, [(i, i ^ mask) for i in range(self.count)])

    def gather(self, values, masks):
        return self.spread([values] * len(masks), masks)

    def spread(self, blocks, masks):
        sent = [self.send(b, m) for b, m in reversed(list(zip(blocks[1:], masks[1:])))]
        return [blocks[0]] + sent[::-1]


def block_of(values, index):
    return lax.dynamic_index_in_dim(values, index, keepdims=False)


def exchange(values, axes):
    return lax.all_to_all(values, axes, split_axis=0, concat_axis=0, tiled=True)


def tie(*values):
    return lax.optimization_barrier(values)


def on_device(
    tokens,
    cotangent,
    lengths,
    in_proj,
    out_proj,
    gate_up,
    down_proj,
    gains_pair,
    in_proj_mom,
    out_proj_mom,
    gate_up_mom,
    down_proj_mom,
    gains_mom,
    in_proj_avg,
    out_proj_avg,
    gate_up_avg,
    down_proj_avg,
    gains_avg,
):
    n_dp, n_z = lax.axis_size("dp"), lax.axis_size("z")
    n_zc = n_z * 2
    links = Links(n_dp, n_z)
    devices = links.count
    at_dp, at_z, at_core = (lax.axis_index(a) for a in AXES)
    at = jnp.stack([at_dp, at_z, at_core]).astype(jnp.int32)
    slots, seq_len = tokens.shape[:2]
    rows = slots * seq_len
    step_rate = RATE_BASE / math.sqrt(slots * devices * seq_len)
    in_width = in_proj.shape[1]
    out_width = out_proj.shape[1]
    ff_width = down_proj.shape[0]
    group = n_zc * in_width
    heads_here = group // HEAD_DIM
    aligned = in_width % 16 == 0 and out_width % 16 == 0

    in_low = low(jnp.transpose(in_proj))
    out_low = low(jnp.transpose(out_proj))
    gain_low = low(gains_pair)
    token_rows = tokens.reshape(rows, D)

    out_z = links.gather(out_low, links.z)
    in_group = lax.all_gather(in_low, ("z", "core"), axis=0, tiled=True)
    token_group = exchange(jnp.tile(token_rows[None], (n_dp, 1, 1)), "dp")
    cos_rows, sine_rows = rotary_rows(seq_len, slots, heads_here)
    head = at_dp * heads_here + jnp.arange(group) // HEAD_DIM
    turned = (head < HEADS + KV_HEADS)[None, :]
    cos_here = jnp.where(turned, cos_rows, 1.0)
    sine_here = jnp.where(turned, sine_rows, 0.0)
    gain_all = jnp.tile(gain_low.reshape(1, -1), (devices, 1))
    gain_all, cos_here, sine_here, cos_rows, sine_rows = tie(
        gain_all, cos_here, sine_here, cos_rows, sine_rows
    )
    row_valid = (jnp.arange(seq_len)[None, :] < lengths[:, None]).reshape(rows, 1)
    upstream = jnp.where(row_valid, cotangent.reshape(rows, D), jnp.zeros((), bf16))
    ff_low, upstream_group = kernel_call(
        pack_body,
        [((3, ff_width, D), bf16), ((n_z, rows, D), bf16)],
        [gate_up, down_proj, upstream],
    )
    gain_all, token_group, upstream_group = tie(gain_all, token_group, upstream_group)
    gain_all = exchange(gain_all, AXES)
    out_own = links.gather(jnp.stack(out_z), links.dp)
    gain_all, in_group = tie(gain_all, in_group)
    ff_low, in_group = tie(ff_low, in_group)
    ff = lax.all_gather(ff_low, PLANE, axis=1, tiled=True)
    upstream_group, in_group = tie(upstream_group, in_group)
    upstream_group = exchange(upstream_group, "z")
    if not aligned:
        gain_all = wide(gain_all).reshape(devices, 2, -1)
        gain_all = jnp.swapaxes(gain_all, 0, 1).reshape(2, D)


    normed_group, gain_rows, *blocks = kernel_call(
        project_body,
        [((n_dp, rows, D), bf16), ((2, D), f32)] + [((rows, group), bf16)] * n_dp,
        [at, token_group, in_group, gain_all, cos_here, sine_here],
        smem=(0,),
        flops=LONG,
    )
    blocks = links.spread(blocks, links.dp)
    normed_group, out_own = tie(normed_group, out_own)

    out_own = jnp.stack(out_own).reshape(n_dp * n_z, out_width, D)
    out_other = links.send(out_own, 1)
    out_parts = [out_own, out_other]
    if not aligned:
        both = jnp.stack(out_parts)
        out_here = at_dp * n_z + at_z
        out_parts = [
            jnp.stack(
                [
                    block_of(block_of(both, at_core ^ c), out_here ^ k)
                    for k in range(n_dp * n_z)
                    for c in range(2)
                ]
            )
        ]

    qkv, prob, attended = kernel_call(
        functools.partial(attend_body, n_dp, slots),
        [
            ((n_dp, rows, group), bf16),
            ((KV_HEADS, GROUPS * rows, rows), f32),
            ((rows, D), bf16),
        ],
        [at, lengths.astype(jnp.int32), *blocks],
        smem=(0, 1),
    )
    attended, upstream_group = tie(attended, upstream_group)
    hidden, normed_two = kernel_call(
        functools.partial(out_body, n_z),
        [((rows, D), f32), ((rows, D), bf16)],
        [at, attended, token_rows, gain_rows, *out_parts],
        smem=(0,),
        hbm=range(4, 4 + len(out_parts)),
        scratch=[((devices, out_width, D), bf16)],
        sems=[()],
    )

    normed_parts = links.gather(normed_two, links.z)
    attended_group = lax.all_gather(attended, "dp", axis=0)
    group_rows, units = n_z * rows, n_dp * 2 * ff_width
    upstream_group, grad_active = kernel_call(
        functools.partial(units_back_body, TILE),
        [((group_rows, D), bf16), ((group_rows, units), f32)],
        [at, upstream_group, ff],
        smem=(0,),
        hbm=(2,),
        scratch=[((units, D), bf16)],
        sems=[(units // TILE,)],
        shared=True,
    )
    out_parts, normed_two = tie(out_parts, normed_two)
    (out_full,) = kernel_call(
        functools.partial(place_body, n_z),
        [((devices, out_width, D), bf16)],
        [at, *out_parts],
        smem=(0,),
        hbm=range(1, 1 + len(out_parts)),
        sems=[()],
    )
    out_full = out_full.reshape(D, D)
    normed_parts, grad_active, out_full = tie(normed_parts, grad_active, out_full)
    normed_rows, active, grad_gate, grad_up, *grad_normed = kernel_call(
        functools.partial(units_body, n_z, TILE),
        [((group_rows, D), bf16)]
        + [((group_rows, units), bf16)] * 3
        + [((rows, D), f32)]
        + [((rows, D), bf16)] * (n_z - 1),
        [*normed_parts, ff, grad_active],
        hbm=range(n_z + 1),
        scratch=[((2, units, D), bf16)],
        sems=[(2, units // TILE), (n_z,)],
        shared=True,
    )
    grad_normed = links.spread(grad_normed, links.z)
    grad_ff, *partial_out = kernel_call(
        functools.partial(units_grad_body, n_z),
        [((3, units, D), bf16), ((rows, D), f32)] + [((rows, D), bf16)] * (n_z - 1),
        [grad_gate, grad_up, active, normed_rows, upstream_group, ff],
        hbm=(5,),
        scratch=[((units, D), bf16)],
        sems=[()],
        shared=True,
    )
    grad_ff = lax.psum_scatter(grad_ff, PLANE, scatter_dimension=1, tiled=True)
    partial_out, grad_normed = tie(partial_out, grad_normed)
    partial_out = links.spread(partial_out, links.z)

    col_width = D // n_dp
    col_aligned = col_width % 128 == 0
    grad_hidden, grad_branch, gain_two_grad, blocks, *columns = kernel_call(
        functools.partial(attend_back_body, n_dp, n_z),
        [((rows, D), f32), ((rows, D), bf16), ((1, D), f32), ((n_dp, rows, group), bf16)]
        + ([((rows, col_width), bf16)] * n_dp if col_aligned else []),
        [
            at,
            *grad_normed,
            hidden,
            gain_rows,
            upstream,
            out_full,
            qkv,
            prob,
            cos_rows,
            sine_rows,
        ],
        smem=(0,),
        late=(*range(2, n_z + 1), *range(n_z + 4, n_z + 9)),
        flops=SHORT,
    )
    if not col_aligned:
        split = jnp.swapaxes(grad_branch.reshape(rows, n_dp, col_width), 0, 1)
        columns = [block_of(split, at_dp ^ k) for k in range(n_dp)]
    columns = links.spread(columns, links.dp)

    blocks, partial_out[-1] = tie(blocks, partial_out[-1])
    grad_proj = exchange(blocks, "dp")
    grad_proj, columns = tie(grad_proj, columns)

    col_rows = in_width + out_width

    if aligned:
        mine, other = kernel_call(
            functools.partial(columns_grad_body, n_dp),
            [((n_z, col_rows, D), f32), ((n_z, col_rows, D), bf16)],
            [at, grad_proj, normed_group, attended_group, *columns],
            scratch=[((n_dp, rows, col_width), bf16), ((n_zc, col_rows, D), f32)],
            smem=(0,),
            late=range(1, n_dp + 4),
            flops=SHORT,
        )
    else:
        columns = jnp.stack(columns)
        columns = jnp.concatenate([block_of(columns, at_dp ^ k) for k in range(n_dp)])
        total = jnp.concatenate(
            [
                dot(lhs.reshape(n_dp * rows, -1), rhs.reshape(-1, D), TN).reshape(n_zc, -1, D)
                for lhs, rhs in ((grad_proj, normed_group), (columns, attended_group))
            ],
            axis=1,
        ).reshape(n_z, 2, col_rows, D)
        mine, other = (
            jnp.stack([block_of(block_of(total, at_z ^ z), at_core ^ c) for z in range(n_z)])
            for c in range(2)
        )
        other = low(other)
    grad_proj, mine = tie(grad_proj, mine)
    other = links.send(other, 1)
    grad_gains, *grad_normed_one = kernel_call(
        inputs_grad_body,
        [((devices, D // devices * 2) if aligned else (2, D), f32), ((rows, D), f32)]
        + [((rows, D), bf16)] * (n_dp - 1),
        [at, grad_proj, in_group, token_group, gain_two_grad],
        smem=(0,),
        flops=SHORT,
    )
    if not aligned:
        grad_gains = jnp.swapaxes(grad_gains.reshape(2, devices, -1), 0, 1).reshape(devices, -1)
    other, partial_out = tie(other, partial_out)
    grad_cols = kernel_call(
        add_body,
        [((col_rows, D), f32)] + [((col_rows, D), bf16)] * (n_z - 1),
        [mine, other],
    )
    grad_normed_one, grad_gains, grad_cols[0] = tie(grad_normed_one, grad_gains, grad_cols[0])
    grad_cols = links.spread(grad_cols, links.z)
    parts = [grad_normed_one[0]]
    for k in range(1, n_dp):
        parts.append(links.send(grad_normed_one[k], links.dp[k]))
    grad_gains = exchange(grad_gains, AXES)
    total_out = hidden + partial_out[0] + sum(wide(r) for r in partial_out[1:])
    produced = low(jnp.where(row_valid, total_out, 0.0))

    grad_normed_one = parts[0] + sum(wide(r) for r in parts[1:])
    inputs = wide(token_rows)
    scale_one = rms_scale(inputs)
    unit_one = inputs * scale_one
    scaled_one = grad_normed_one * gain_rows[0:1]
    grad_inputs = grad_hidden + scale_one * (
        scaled_one - unit_one * jnp.mean(scaled_one * unit_one, axis=-1, keepdims=True)
    )


    def settle(grads, *state):
        state = [jnp.transpose(v) for v in state]
        outs = kernel_call(
            functools.partial(settle_body, step_rate, len(grads)),
            [(v.shape, t) for v in state[::3] for t in (f32, f32, f32, f32, bf16)],
            [*grads, *state],
        )
        return [jnp.transpose(v) for v in outs]

    state = [gate_up, gate_up_mom, gate_up_avg, down_proj, down_proj_mom, down_proj_avg]
    new_ff = kernel_call(
        functools.partial(update_body, step_rate),
        [(v.shape, t) for v in state[::3] for t in (f32, f32, f32, f32, bf16)],
        [grad_ff, *state],
    )
    grad_cols, grad_gains, new_ff = tie(grad_cols, grad_gains, new_ff)
    grad_gain = jnp.sum(grad_gains, axis=0).reshape(gains_pair.shape)
    new_gains = update(gains_pair, grad_gain, gains_mom, gains_avg, step_rate)
    new_cols = settle(
        grad_cols, in_proj, in_proj_mom, in_proj_avg, out_proj, out_proj_mom, out_proj_avg
    )
    return (
        produced.reshape(tokens.shape),
        grad_inputs.reshape(tokens.shape),
        *new_cols,
        *new_ff,
        *new_gains,
    )


def solution(mesh):
    n_dp, n_fsdp = mesh.devices.shape
    fine = Mesh(mesh.devices.reshape(n_dp, n_fsdp // 2, 2), AXES)
    rows = P(AXES, None, None)
    last_of_two = P(None, AXES)
    first_of_two = P(AXES, None)
    last_of_three = P(None, None, AXES)
    weights = (last_of_two, last_of_two, last_of_three, first_of_two, last_of_two)
    in_specs = (rows, rows, P(AXES)) + weights * 3
    out_specs = (rows, rows) + tuple(spec for spec in weights for _ in range(5))
    return jax.shard_map(
        on_device, mesh=fine, in_specs=in_specs, out_specs=out_specs, check_vma=False
    )
```

```python
import functools
import math

import jax
import jax.numpy as jnp
from jax import lax
from jax.experimental import pallas as pl
from jax.experimental.pallas import tpu as pltpu
from jax.sharding import Mesh
from jax.sharding import PartitionSpec as P

D = 1536
HEADS = 16
KV_HEADS = 8
HEAD_DIM = 96
HALF = HEAD_DIM // 2
ALL_HEADS = HEADS + 2 * KV_HEADS
GROUPS = HEADS // KV_HEADS

EPS = 1e-05
THETA = 10000.0
MASKED = -1e30
MOMENTUM_RATE = 0.9
AVERAGE_RATE = 0.75
RATE_BASE = 0.1
AXES = ("dp", "z", "core")
PLANE = ("dp", "core")
NN = (((1,), (0,)), ((), ()))
TN = (((0,), (0,)), ((), ()))
NT = (((1,), (1,)), ((), ()))
VMEM_SLACK = 12 * 1024 * 1024
VMEM_ALL = 60 * 1024 * 1024
TILE = 256
SHORT = 30_000_000_000
LONG = 300_000_000_000

bf16 = jnp.bfloat16
f32 = jnp.float32


def dot(a, b, dims):
    return lax.dot_general(a, b, dims, preferred_element_type=f32)


def low(values):
    return values.astype(bf16)


def wide(values):
    return values.astype(f32)


def rms_scale(values):
    return lax.rsqrt(jnp.mean(values * values, axis=-1, keepdims=True) + EPS)


def rotary_rows(seq_len, slots, heads):
    positions = jnp.arange(seq_len, dtype=f32)
    halves = jnp.arange(HALF, dtype=f32)
    frequencies = jnp.power(THETA, -2.0 * halves / HEAD_DIM)
    angles = positions[:, None] * frequencies[None, :]
    cos_table, sine_table = jnp.cos(angles), jnp.sin(angles)
    cos_rows = jnp.concatenate([cos_table, cos_table], axis=1)
    sine_rows = jnp.concatenate([-sine_table, sine_table], axis=1)
    return jnp.tile(cos_rows, (slots, heads)), jnp.tile(sine_rows, (slots, heads))


def swap_halves(values):
    width = values.shape[1]
    if width % 128 == 0:
        left = pltpu.roll(values, width - HALF, 1)
        right = pltpu.roll(values, HALF, 1)
    else:
        left = jnp.concatenate([values[:, HALF:], values[:, :HALF]], axis=1)
        right = jnp.concatenate([values[:, -HALF:], values[:, :-HALF]], axis=1)
    column = lax.broadcasted_iota(jnp.int32, values.shape, 1)
    return jnp.where(lax.rem(column, HEAD_DIM) < HALF, left, right)


def waited(copy, ref):
    copy.wait()
    return ref


def kernel_call(
    body, outs, ins, smem=(), hbm=(), late=(), far=(), scratch=(), sems=(), shared=False, flops=0
):
    moved = [i for i in range(len(ins)) if i not in smem and i not in hbm]

    def fetched(*refs):
        given, rest = list(refs[: len(ins)]), refs[len(ins) :]
        held, sems = rest[-1 - len(moved) : -1], rest[-1]
        copies = [
            pltpu.make_async_copy(given[i], held[j], sems.at[j]) for j, i in enumerate(moved)
        ]
        for copy in copies:
            copy.start()
        for j, i in enumerate(moved):
            given[i] = held[j]
            if i in late:
                given[i] = functools.partial(waited, copies[j], held[j])
            else:
                copies[j].wait()
        body(*given, *rest[: -1 - len(moved)])

    arrays = [v for i, v in enumerate(outs) if i not in far]
    arrays += [*((ins[i].shape, ins[i].dtype) for i in moved)]
    arrays += scratch
    held_bytes = sum(math.prod(s) * jnp.dtype(t).itemsize for s, t in arrays)
    outputs = pl.pallas_call(
        fetched,
        out_shape=[jax.ShapeDtypeStruct(s, t) for s, t in outs],
        in_specs=[
            pl.BlockSpec(memory_space=pltpu.SMEM if i in smem else pltpu.HBM)
            for i in range(len(ins))
        ],
        out_specs=[
            pl.BlockSpec(memory_space=pltpu.HBM if i in far else pltpu.VMEM)
            for i in range(len(outs))
        ],
        scratch_shapes=[
            *(pltpu.VMEM(s, t) for s, t in scratch),
            *(pltpu.SemaphoreType.DMA(s) for s in sems),
            *(pltpu.VMEM(ins[i].shape, ins[i].dtype) for i in moved),
            pltpu.SemaphoreType.DMA((len(moved),)),
        ],
        compiler_params=pltpu.CompilerParams(vmem_limit_bytes=held_bytes + VMEM_SLACK if shared else VMEM_ALL),
        cost_estimate=pl.CostEstimate(flops=flops, bytes_accessed=0, transcendentals=0),
    )(*ins)
    return list(outputs)


def project_body(at_ref, x_ref, w_ref, gains_ref, cos_ref, sine_ref, normed_ref, rows_ref, *refs):
    if gains_ref.shape[1] == D:
        rows_ref[...] = gains_ref[...]
    else:
        gains = wide(gains_ref[...])
        width = gains.shape[1] // 2
        for i in range(2):
            rows_ref[i : i + 1, :] = jnp.concatenate(
                [
                    gains[d : d + 1, i * width : (i + 1) * width]
                    for d in range(gains.shape[0])
                ],
                axis=1,
            )
    for k, ref in enumerate(refs):
        x = wide(x_ref[at_ref[0] ^ k])
        normed = low(x * rms_scale(x) * rows_ref[0:1, :])
        normed_ref[at_ref[0] ^ k] = normed
        p = dot(normed, w_ref[...], NT)
        ref[...] = low(p * cos_ref[...] + swap_halves(p) * sine_ref[...])


def head_columns(blocks_ref, head):
    per = blocks_ref.shape[2] // HEAD_DIM
    at = (head % per) * HEAD_DIM
    return blocks_ref[head // per, :, at : at + HEAD_DIM]


def attend_body(n, slots, at_ref, len_ref, *refs):
    in_refs, (qkv_ref, prob_ref, att_ref) = refs[:n], refs[n:]
    for k in range(n):
        qkv_ref[at_ref[0] ^ k] = in_refs[k][...]
    rows = qkv_ref.shape[1]
    seq_len = rows // slots
    shape = (GROUPS * rows, rows)
    row = lax.rem(lax.broadcasted_iota(jnp.int32, shape, 0), rows)
    col = lax.broadcasted_iota(jnp.int32, shape, 1)
    limit = jnp.zeros(shape, jnp.int32)
    for b in range(slots):
        limit = jnp.where(row >= b * seq_len, b * seq_len + len_ref[b], limit)
    first = row - lax.rem(row, seq_len)
    allowed = (col >= first) & (col <= row) & (col < limit)
    outs = []
    for g in range(KV_HEADS):
        q = jnp.concatenate([head_columns(qkv_ref, GROUPS * g + i) for i in range(GROUPS)], axis=0)
        k = head_columns(qkv_ref, HEADS + g)
        v = head_columns(qkv_ref, HEADS + KV_HEADS + g)
        s = jnp.where(allowed, dot(q, k, NT) * HEAD_DIM ** (-0.5), MASKED)
        e = jnp.exp(s - jnp.max(s, axis=-1, keepdims=True))
        p = e / jnp.sum(e, axis=-1, keepdims=True)
        prob_ref[g] = p
        o = dot(low(p), v, NN)
        outs += [o[i * rows : (i + 1) * rows] for i in range(GROUPS)]
    att_ref[...] = low(jnp.concatenate(outs, axis=1))


def place_copies(n_z, at_ref, parts, wo_ref, sem):
    if len(parts) == 1:
        return [pltpu.make_async_copy(parts[0], wo_ref, sem)]
    copies = []
    for c, part in enumerate(parts):
        for k in range(part.shape[0]):
            to = (at_ref[0] ^ (k // n_z)) * n_z + (at_ref[1] ^ (k % n_z))
            to = to * 2 + (at_ref[2] ^ c)
            copies.append(pltpu.make_async_copy(part.at[k], wo_ref.at[to], sem))
    return copies


def place_body(n_z, at_ref, *refs):
    copies = place_copies(n_z, at_ref, refs[:-2], refs[-2], refs[-1])
    for copy in copies:
        copy.start()
    for copy in copies:
        copy.wait()


def out_body(n_z, at_ref, att_ref, x_ref, gain_ref, *refs):
    parts, (hidden_ref, normed_ref, wo_ref, sem) = refs[:-4], refs[-4:]
    copies = place_copies(n_z, at_ref, parts, wo_ref, sem)
    for copy in copies:
        copy.start()
    for copy in copies:
        copy.wait()
    hidden = wide(x_ref[...]) + dot(att_ref[...], wo_ref[...].reshape(D, D), NT)
    hidden_ref[...] = hidden
    normed_ref[...] = low(hidden * rms_scale(hidden) * gain_ref[1:2, :])


def units_back_body(tile, at_ref, dy_ref, w_ref, rows_ref, out_ref, held_ref, sems):
    tiles = range(0, held_ref.shape[0], tile)
    copies = [
        pltpu.make_async_copy(
            w_ref.at[2, pl.ds(j, tile)], held_ref.at[pl.ds(j, tile)], sems.at[i]
        )
        for i, j in enumerate(tiles)
    ]
    for copy in copies:
        copy.start()
    rows = dy_ref.shape[1]
    for k in range(dy_ref.shape[0]):
        rows_ref[k * rows : (k + 1) * rows, :] = dy_ref[at_ref[1] ^ k]
    for copy, j in zip(copies, tiles):
        copy.wait()
        out_ref[:, j : j + tile] = dot(rows_ref[...], held_ref[j : j + tile, :], NT)


def units_body(n, tile, *refs):
    n2_refs, (w_ref, da_ref) = refs[:n], refs[n : n + 2]
    rows_ref, act_ref, gate_ref, up_ref = refs[n + 2 : n + 6]
    own_ref, out_refs = refs[n + 6], refs[n + 7 : 2 * n + 6]
    held_ref, sems, row_sems = refs[2 * n + 6 :]
    tiles = range(0, held_ref.shape[1], tile)
    copies = [
        [
            pltpu.make_async_copy(
                w_ref.at[p, pl.ds(j, tile)], held_ref.at[p, pl.ds(j, tile)], sems.at[p, i]
            )
            for p in range(2)
        ]
        for i, j in enumerate(tiles)
    ]
    for pair in copies:
        for copy in pair:
            copy.start()
    rows = n2_refs[0].shape[0]
    moves = [
        pltpu.make_async_copy(n2_refs[k], rows_ref.at[pl.ds(k * rows, rows)], row_sems.at[k])
        for k in range(n)
    ]
    for move in moves:
        move.start()
    for move in moves:
        move.wait()
    for pair, j in zip(copies, tiles):
        for copy in pair:
            copy.wait()
        at = slice(j, j + tile)
        gate = dot(rows_ref[...], held_ref[0, at, :], NT)
        up = dot(rows_ref[...], held_ref[1, at, :], NT)
        da = da_ref[:, at]
        sig = jax.nn.sigmoid(gate)
        silu = gate * sig
        act_ref[:, at] = low(silu * up)
        gate_ref[:, at] = low(da * up * sig * (1.0 + gate * (1.0 - sig)))
        up_ref[:, at] = low(da * silu)
    for j in range(0, D, tile):
        at = slice(j, j + tile)
        back = dot(gate_ref[...], held_ref[0, :, at], NN) + dot(
            up_ref[...], held_ref[1, :, at], NN
        )
        own_ref[:, at] = back[:rows]
        for k in range(1, n):
            out_refs[k - 1][:, at] = low(back[k * rows : (k + 1) * rows])


def attend_back_body(n, n_z, at_ref, own_ref, *refs):
    got = refs[: n_z - 1]
    hidden_ref, gain_ref, up_ref, late_wo, late_qkv, late_prob, late_cos, late_sine = refs[
        n_z - 1 : n_z + 7
    ]
    grad_ref, low_ref, gain_grad_ref, heads_ref = refs[n_z + 7 : n_z + 11]
    col_refs = refs[n_z + 11 :]
    hidden = hidden_ref[...]
    scale = rms_scale(hidden)
    unit = hidden * scale
    dn = own_ref[...]
    for late in got:
        dn = dn + wide(late()[...])
    gain_grad_ref[...] = jnp.sum(dn * unit, axis=0, keepdims=True)
    scaled = dn * gain_ref[1:2, :]
    grad = wide(up_ref[...]) + scale * (
        scaled - unit * jnp.mean(scaled * unit, axis=-1, keepdims=True)
    )
    grad_ref[...] = grad
    low_ref[...] = low(grad)
    width = D // n
    for k, ref in enumerate(col_refs):
        at = pl.multiple_of((at_ref[0] ^ k) * width, 128)
        ref[...] = low_ref[:, pl.ds(at, width)]

    wo_ref = late_wo()
    do = low(dot(low_ref[...], wo_ref[...], NN))
    qkv_ref, prob_ref, cos_ref, sine_ref = late_qkv(), late_prob(), late_cos(), late_sine()
    rows = do.shape[0]
    grads = [None] * ALL_HEADS
    root = HEAD_DIM ** (-0.5)
    for g in range(KV_HEADS):
        q = jnp.concatenate([head_columns(qkv_ref, GROUPS * g + i) for i in range(GROUPS)], axis=0)
        k = head_columns(qkv_ref, HEADS + g)
        v = head_columns(qkv_ref, HEADS + KV_HEADS + g)
        d = jnp.concatenate(
            [
                do[:, h * HEAD_DIM : (h + 1) * HEAD_DIM]
                for h in range(GROUPS * g, GROUPS * g + GROUPS)
            ],
            axis=0,
        )
        p = prob_ref[g]
        dp = dot(d, v, NT)
        ds = low(p * (dp - jnp.sum(p * dp, axis=-1, keepdims=True)))
        dq = dot(ds, k, NN) * root
        for i in range(GROUPS):
            grads[GROUPS * g + i] = dq[i * rows : (i + 1) * rows]
        grads[HEADS + g] = dot(ds, q, TN) * root
        grads[HEADS + KV_HEADS + g] = dot(low(p), d, TN)
    per = ALL_HEADS // n
    for j in range(n):
        block = jnp.concatenate(grads[j * per : (j + 1) * per], axis=1)
        turned = max(0, min(per, HEADS + KV_HEADS - j * per))
        if turned:
            back = block * cos_ref[...] - swap_halves(block) * sine_ref[...]
            if turned < per:
                column = lax.broadcasted_iota(jnp.int32, block.shape, 1)
                back = jnp.where(column < turned * HEAD_DIM, back, block)
            block = back
        heads_ref[j] = low(block)


def units_grad_body(n, gate_ref, up_ref, act_ref, rows_ref, dy_ref, w_ref, *refs):
    out_ref, own_ref, part_refs = refs[0], refs[1], refs[2 : n + 1]
    held_ref, sem = refs[n + 1 :]
    copy = pltpu.make_async_copy(w_ref.at[2], held_ref, sem)
    copy.start()
    for j in range(0, gate_ref.shape[1], TILE):
        at = slice(j, j + TILE)
        out_ref[0, at, :] = low(dot(gate_ref[:, at], rows_ref[...], TN))
        out_ref[1, at, :] = low(dot(up_ref[:, at], rows_ref[...], TN))
        out_ref[2, at, :] = low(dot(act_ref[:, at], dy_ref[...], TN))
    copy.wait()
    rows = own_ref.shape[0]
    for j in range(0, D, TILE):
        at = slice(j, j + TILE)
        out = dot(act_ref[...], held_ref[:, at], NN)
        own_ref[:, at] = out[:rows]
        for k in range(1, n):
            part_refs[k - 1][:, at] = low(out[k * rows : (k + 1) * rows])


def columns_grad_body(n, at_ref, late_in, late_normed, late_att, *refs):
    late_cols, (mine_ref, other_ref, held_ref, sum_ref) = refs[:n], refs[n:]
    n_z = mine_ref.shape[0]
    blocks = 2 * n_z
    in_ref, normed_ref = late_in(), late_normed()
    grads = in_ref[...].reshape(-1, in_ref.shape[2])
    normed = normed_ref[...].reshape(-1, D)
    first = grads.shape[1] // blocks
    for j in range(0, D, 512):
        at = slice(j, j + 512)
        one = dot(grads, normed[:, at], TN)
        for i in range(blocks):
            sum_ref[i, :first, at] = one[i * first : (i + 1) * first]
    for k in range(n):
        held_ref[at_ref[0] ^ k] = late_cols[k]()[...]
    cols = held_ref[...].reshape(-1, held_ref.shape[2])
    att = late_att()[...].reshape(-1, D)
    second = cols.shape[1] // blocks
    for j in range(0, D, 512):
        at = slice(j, j + 512)
        two = dot(cols, att[:, at], TN)
        for i in range(blocks):
            sum_ref[i, first:, at] = two[i * second : (i + 1) * second]
    for z in range(n_z):
        i = (at_ref[1] ^ z) * 2
        mine_ref[z] = sum_ref[i + at_ref[2]]
        other_ref[z] = low(sum_ref[i + (at_ref[2] ^ 1)])


def add_body(mine_ref, other_ref, own_ref, *out_refs):
    own_ref[...] = mine_ref[0] + wide(other_ref[0])
    for k, ref in enumerate(out_refs):
        ref[...] = low(mine_ref[k + 1] + wide(other_ref[k + 1]))


def inputs_grad_body(at_ref, grad_ref, w_ref, x_ref, second_ref, gain_ref, *out_refs):
    total = jnp.zeros((1, D), f32)
    for k, ref in enumerate(out_refs):
        back = dot(grad_ref[at_ref[0] ^ k], w_ref[...], NN)
        x = wide(x_ref[at_ref[0] ^ k])
        total = total + jnp.sum(back * (x * rms_scale(x)), axis=0, keepdims=True)
        ref[...] = back.astype(ref.dtype)
    if gain_ref.shape[1] == D:
        gain_ref[0:1, :] = total
        gain_ref[1:2, :] = second_ref[...]
    else:
        width = gain_ref.shape[1] // 2
        for d in range(gain_ref.shape[0]):
            at = slice(d * width, (d + 1) * width)
            gain_ref[d : d + 1, :width] = total[:, at]
            gain_ref[d : d + 1, width:] = second_ref[:, at]


def settle_body(rate, n, *refs):
    grad_refs, refs = refs[:n], refs[n:]
    at = 0
    for ins, outs in ((refs[0:3], refs[6:11]), (refs[3:6], refs[11:16])):
        weight, moment, average = (r[...] for r in ins)
        gradient = sum(wide(r[at : at + weight.shape[0], :]) for r in grad_refs)
        at += weight.shape[0]
        for ref, value in zip(outs, update(weight, gradient, moment, average, rate)):
            ref[...] = value


def pack_body(gate_ref, down_ref, up_ref, out_ref, copies_ref):
    for k in range(copies_ref.shape[0]):
        copies_ref[k] = up_ref[...]
    out_ref[0] = low(gate_ref[0].T)
    out_ref[1] = low(gate_ref[1].T)
    out_ref[2] = low(down_ref[...])


def update_body(rate, grad_ref, *refs):
    ins, outs = refs[:6], refs[6:]
    for p in range(2):
        weight, moment, average = (r[p] for r in ins[:3])
        gradient = wide(grad_ref[p].T)
        for ref, value in zip(outs[:5], update(weight, gradient, moment, average, rate)):
            ref[p] = value
    weight, moment, average = (r[...] for r in ins[3:])
    for ref, value in zip(outs[5:], update(weight, wide(grad_ref[2]), moment, average, rate)):
        ref[...] = value


def update(weight, gradient, moment, average, step_rate):
    moment_new = MOMENTUM_RATE * moment + gradient
    weight_new = weight - step_rate * (gradient + MOMENTUM_RATE * moment_new)
    average_new = AVERAGE_RATE * average + (1.0 - AVERAGE_RATE) * weight_new
    return (gradient, moment_new, weight_new, average_new, weight_new.astype(bf16))


class Links:
    def __init__(self, n_dp, n_z):
        assert n_dp & (n_dp - 1) == 0 and n_z & (n_z - 1) == 0
        self.count = n_dp * n_z * 2
        self.dp = [n_z * 2 * k for k in range(n_dp)]
        self.z = [2 * k for k in range(n_z)]

    def send(self, values, mask):
        return lax.ppermute(values, AXES, [(i, i ^ mask) for i in range(self.count)])

    def gather(self, values, masks):
        return self.spread([values] * len(masks), masks)

    def spread(self, blocks, masks):
        sent = [self.send(b, m) for b, m in reversed(list(zip(blocks[1:], masks[1:])))]
        return [blocks[0]] + sent[::-1]


def block_of(values, index):
    return lax.dynamic_index_in_dim(values, index, keepdims=False)


def exchange(values, axes):
    return lax.all_to_all(values, axes, split_axis=0, concat_axis=0, tiled=True)


def tie(*values):
    return lax.optimization_barrier(values)


def on_device(
    tokens,
    cotangent,
    lengths,
    in_proj,
    out_proj,
    gate_up,
    down_proj,
    gains_pair,
    in_proj_mom,
    out_proj_mom,
    gate_up_mom,
    down_proj_mom,
    gains_mom,
    in_proj_avg,
    out_proj_avg,
    gate_up_avg,
    down_proj_avg,
    gains_avg,
):
    n_dp, n_z = lax.axis_size("dp"), lax.axis_size("z")
    n_zc = n_z * 2
    links = Links(n_dp, n_z)
    devices = links.count
    at_dp, at_z, at_core = (lax.axis_index(a) for a in AXES)
    at = jnp.stack([at_dp, at_z, at_core]).astype(jnp.int32)
    slots, seq_len = tokens.shape[:2]
    rows = slots * seq_len
    step_rate = RATE_BASE / math.sqrt(slots * devices * seq_len)
    in_width = in_proj.shape[1]
    out_width = out_proj.shape[1]
    ff_width = down_proj.shape[0]
    group = n_zc * in_width
    heads_here = group // HEAD_DIM
    aligned = in_width % 16 == 0 and out_width % 16 == 0

    in_low = low(jnp.transpose(in_proj))
    out_low = low(jnp.transpose(out_proj))
    gain_low = low(gains_pair)
    token_rows = tokens.reshape(rows, D)

    token_copies = jnp.tile(token_rows[None], (n_dp, 1, 1))
    out_low, token_copies = tie(out_low, token_copies)
    out_z = links.gather(out_low, links.z)
    in_group = lax.all_gather(in_low, ("z", "core"), axis=0, tiled=True)
    token_group = exchange(token_copies, "dp")
    cos_rows, sine_rows = rotary_rows(seq_len, slots, heads_here)
    head = at_dp * heads_here + jnp.arange(group) // HEAD_DIM
    turned = (head < HEADS + KV_HEADS)[None, :]
    cos_here = jnp.where(turned, cos_rows, 1.0)
    sine_here = jnp.where(turned, sine_rows, 0.0)
    gain_all = jnp.tile(gain_low.reshape(1, -1), (devices, 1))
    gain_all, cos_here, sine_here, cos_rows, sine_rows = tie(
        gain_all, cos_here, sine_here, cos_rows, sine_rows
    )
    row_valid = (jnp.arange(seq_len)[None, :] < lengths[:, None]).reshape(rows, 1)
    upstream = jnp.where(row_valid, cotangent.reshape(rows, D), jnp.zeros((), bf16))
    ff_low, upstream_group = kernel_call(
        pack_body,
        [((3, ff_width, D), bf16), ((n_z, rows, D), bf16)],
        [gate_up, down_proj, upstream],
    )
    gain_all, token_group, upstream_group = tie(gain_all, token_group, upstream_group)
    gain_all = exchange(gain_all, AXES)
    out_own = links.gather(jnp.stack(out_z), links.dp)
    gain_all, in_group = tie(gain_all, in_group)
    ff_low, in_group = tie(ff_low, in_group)
    ff = lax.all_gather(ff_low, PLANE, axis=1, tiled=True)
    upstream_group, in_group = tie(upstream_group, in_group)
    upstream_group = exchange(upstream_group, "z")
    if not aligned:
        gain_all = wide(gain_all).reshape(devices, 2, -1)
        gain_all = jnp.swapaxes(gain_all, 0, 1).reshape(2, D)


    normed_group, gain_rows, *blocks = kernel_call(
        project_body,
        [((n_dp, rows, D), bf16), ((2, D), f32)] + [((rows, group), bf16)] * n_dp,
        [at, token_group, in_group, gain_all, cos_here, sine_here],
        smem=(0,),
        flops=LONG,
    )
    blocks = links.spread(blocks, links.dp)
    normed_group, out_own = tie(normed_group, out_own)

    out_own = jnp.stack(out_own).reshape(n_dp * n_z, out_width, D)
    out_other = links.send(out_own, 1)
    out_parts = [out_own, out_other]
    if not aligned:
        both = jnp.stack(out_parts)
        out_here = at_dp * n_z + at_z
        out_parts = [
            jnp.stack(
                [
                    block_of(block_of(both, at_core ^ c), out_here ^ k)
                    for k in range(n_dp * n_z)
                    for c in range(2)
                ]
            )
        ]

    qkv, prob, attended = kernel_call(
        functools.partial(attend_body, n_dp, slots),
        [
            ((n_dp, rows, group), bf16),
            ((KV_HEADS, GROUPS * rows, rows), f32),
            ((rows, D), bf16),
        ],
        [at, lengths.astype(jnp.int32), *blocks],
        smem=(0, 1),
    )
    attended, upstream_group = tie(attended, upstream_group)
    hidden, normed_two = kernel_call(
        functools.partial(out_body, n_z),
        [((rows, D), f32), ((rows, D), bf16)],
        [at, attended, token_rows, gain_rows, *out_parts],
        smem=(0,),
        hbm=range(4, 4 + len(out_parts)),
        scratch=[((devices, out_width, D), bf16)],
        sems=[()],
    )

    normed_parts = links.gather(normed_two, links.z)
    attended_group = lax.all_gather(attended, "dp", axis=0)
    group_rows, units = n_z * rows, n_dp * 2 * ff_width
    upstream_group, grad_active = kernel_call(
        functools.partial(units_back_body, TILE),
        [((group_rows, D), bf16), ((group_rows, units), f32)],
        [at, upstream_group, ff],
        smem=(0,),
        hbm=(2,),
        scratch=[((units, D), bf16)],
        sems=[(units // TILE,)],
        shared=True,
    )
    out_parts, normed_two = tie(out_parts, normed_two)
    (out_full,) = kernel_call(
        functools.partial(place_body, n_z),
        [((devices, out_width, D), bf16)],
        [at, *out_parts],
        smem=(0,),
        hbm=range(1, 1 + len(out_parts)),
        sems=[()],
    )
    out_full = out_full.reshape(D, D)
    normed_parts, grad_active, out_full = tie(normed_parts, grad_active, out_full)
    normed_rows, active, grad_gate, grad_up, *grad_normed = kernel_call(
        functools.partial(units_body, n_z, TILE),
        [((group_rows, D), bf16)]
        + [((group_rows, units), bf16)] * 3
        + [((rows, D), f32)]
        + [((rows, D), bf16)] * (n_z - 1),
        [*normed_parts, ff, grad_active],
        hbm=range(n_z + 1),
        scratch=[((2, units, D), bf16)],
        sems=[(2, units // TILE), (n_z,)],
        shared=True,
    )
    grad_normed = links.spread(grad_normed, links.z)
    grad_ff, *partial_out = kernel_call(
        functools.partial(units_grad_body, n_z),
        [((3, units, D), bf16), ((rows, D), f32)] + [((rows, D), bf16)] * (n_z - 1),
        [grad_gate, grad_up, active, normed_rows, upstream_group, ff],
        hbm=(5,),
        scratch=[((units, D), bf16)],
        sems=[()],
        shared=True,
    )
    grad_ff = lax.psum_scatter(grad_ff, PLANE, scatter_dimension=1, tiled=True)
    partial_out, grad_normed = tie(partial_out, grad_normed)
    partial_out = links.spread(partial_out, links.z)

    col_width = D // n_dp
    col_aligned = col_width % 128 == 0
    grad_hidden, grad_branch, gain_two_grad, blocks, *columns = kernel_call(
        functools.partial(attend_back_body, n_dp, n_z),
        [((rows, D), f32), ((rows, D), bf16), ((1, D), f32), ((n_dp, rows, group), bf16)]
        + ([((rows, col_width), bf16)] * n_dp if col_aligned else []),
        [
            at,
            *grad_normed,
            hidden,
            gain_rows,
            upstream,
            out_full,
            qkv,
            prob,
            cos_rows,
            sine_rows,
        ],
        smem=(0,),
        late=(*range(2, n_z + 1), *range(n_z + 4, n_z + 9)),
        flops=SHORT,
    )
    if not col_aligned:
        split = jnp.swapaxes(grad_branch.reshape(rows, n_dp, col_width), 0, 1)
        columns = [block_of(split, at_dp ^ k) for k in range(n_dp)]
    columns = links.spread(columns, links.dp)

    blocks, partial_out[-1] = tie(blocks, partial_out[-1])
    grad_proj = exchange(blocks, "dp")
    grad_proj, columns = tie(grad_proj, columns)

    col_rows = in_width + out_width

    if aligned:
        mine, other = kernel_call(
            functools.partial(columns_grad_body, n_dp),
            [((n_z, col_rows, D), f32), ((n_z, col_rows, D), bf16)],
            [at, grad_proj, normed_group, attended_group, *columns],
            scratch=[((n_dp, rows, col_width), bf16), ((n_zc, col_rows, D), f32)],
            smem=(0,),
            late=range(1, n_dp + 4),
            flops=SHORT,
        )
    else:
        columns = jnp.stack(columns)
        columns = jnp.concatenate([block_of(columns, at_dp ^ k) for k in range(n_dp)])
        total = jnp.concatenate(
            [
                dot(lhs.reshape(n_dp * rows, -1), rhs.reshape(-1, D), TN).reshape(n_zc, -1, D)
                for lhs, rhs in ((grad_proj, normed_group), (columns, attended_group))
            ],
            axis=1,
        ).reshape(n_z, 2, col_rows, D)
        mine, other = (
            jnp.stack([block_of(block_of(total, at_z ^ z), at_core ^ c) for z in range(n_z)])
            for c in range(2)
        )
        other = low(other)
    grad_proj, mine = tie(grad_proj, mine)
    other = links.send(other, 1)
    grad_gains, *grad_normed_one = kernel_call(
        inputs_grad_body,
        [((devices, D // devices * 2) if aligned else (2, D), f32), ((rows, D), f32)]
        + [((rows, D), bf16)] * (n_dp - 1),
        [at, grad_proj, in_group, token_group, gain_two_grad],
        smem=(0,),
        flops=SHORT,
    )
    if not aligned:
        grad_gains = jnp.swapaxes(grad_gains.reshape(2, devices, -1), 0, 1).reshape(devices, -1)
    other, partial_out = tie(other, partial_out)
    grad_cols = kernel_call(
        add_body,
        [((col_rows, D), f32)] + [((col_rows, D), bf16)] * (n_z - 1),
        [mine, other],
    )
    grad_normed_one, grad_gains, grad_cols[0] = tie(grad_normed_one, grad_gains, grad_cols[0])
    grad_cols = links.spread(grad_cols, links.z)
    parts = [grad_normed_one[0]]
    for k in range(1, n_dp):
        parts.append(links.send(grad_normed_one[k], links.dp[k]))
    grad_gains = exchange(grad_gains, AXES)
    total_out = hidden + partial_out[0] + sum(wide(r) for r in partial_out[1:])
    produced = low(jnp.where(row_valid, total_out, 0.0))

    grad_normed_one = parts[0] + sum(wide(r) for r in parts[1:])
    inputs = wide(token_rows)
    scale_one = rms_scale(inputs)
    unit_one = inputs * scale_one
    scaled_one = grad_normed_one * gain_rows[0:1]
    grad_inputs = grad_hidden + scale_one * (
        scaled_one - unit_one * jnp.mean(scaled_one * unit_one, axis=-1, keepdims=True)
    )


    def settle(grads, *state):
        state = [jnp.transpose(v) for v in state]
        outs = kernel_call(
            functools.partial(settle_body, step_rate, len(grads)),
            [(v.shape, t) for v in state[::3] for t in (f32, f32, f32, f32, bf16)],
            [*grads, *state],
        )
        return [jnp.transpose(v) for v in outs]

    state = [gate_up, gate_up_mom, gate_up_avg, down_proj, down_proj_mom, down_proj_avg]
    new_ff = kernel_call(
        functools.partial(update_body, step_rate),
        [(v.shape, t) for v in state[::3] for t in (f32, f32, f32, f32, bf16)],
        [grad_ff, *state],
    )
    grad_cols, grad_gains, new_ff = tie(grad_cols, grad_gains, new_ff)
    grad_gain = jnp.sum(grad_gains, axis=0).reshape(gains_pair.shape)
    new_gains = update(gains_pair, grad_gain, gains_mom, gains_avg, step_rate)
    new_cols = settle(
        grad_cols, in_proj, in_proj_mom, in_proj_avg, out_proj, out_proj_mom, out_proj_avg
    )
    return (
        produced.reshape(tokens.shape),
        grad_inputs.reshape(tokens.shape),
        *new_cols,
        *new_ff,
        *new_gains,
    )


def solution(mesh):
    n_dp, n_fsdp = mesh.devices.shape
    fine = Mesh(mesh.devices.reshape(n_dp, n_fsdp // 2, 2), AXES)
    rows = P(AXES, None, None)
    last_of_two = P(None, AXES)
    first_of_two = P(AXES, None)
    last_of_three = P(None, None, AXES)
    weights = (last_of_two, last_of_two, last_of_three, first_of_two, last_of_two)
    in_specs = (rows, rows, P(AXES)) + weights * 3
    out_specs = (rows, rows) + tuple(spec for spec in weights for _ in range(5))
    return jax.shard_map(
        on_device, mesh=fine, in_specs=in_specs, out_specs=out_specs, check_vma=False
    )
```
